512 devices in a mesh: wave: 64 (over z, y), lev: 8 (over x, core).
Axes of the slice: x: 4, y: 8, z: 8, core: 2. Of those that a mesh axis runs over, the one named last changes fastest.
Arguments:
- fourier_in: bfloat16 [2, 32, 2560, 256], P(None, 'lev', 'wave'), may hold values from -6 to 6
- table: bfloat16 [64, 1281, 2560], P('wave', None, 'lev'), may hold values from -0.125 to 0.125
- points: int32 [2560], replicated, may hold values from 20 to 5136, as said below
- pair_low: int32 [64], P('wave'), may hold values from 0 to 639, as said below
- gamma: float32 [32], replicated, may hold values from 1 to 100
- beta: float32 [32], replicated, may hold values from 0.5 to 2
Outputs:
- fourier_out: bfloat16 [2, 32, 2560, 256], P(None, 'lev', 'wave')
The draws below stay inside these ranges and needn't reach their ends.
Inputs may be any that keep to these rules, and one draw needn't show every extreme that they name: `points`: each is a multiple of 4; row i has at most 20 + 4 min(i, 2559 - i) points and at most 32 fewer; the two middle rows have exactly the most. `pair_low`: all distinct.
All inputs are finite; a program needn't handle non-finite values.
Results may differ from the reference program's by a relative error of at most 0.0055.
Values may be sent and summed in bfloat16 or wider, within the bound.
No kernel may reach another device: no remote copies, remote signals or barrier semaphores. Data moves between devices by JAX's collectives and lax.ppermute only.
A program may use at most 64 MiB of HBM per device.

```python
import math
import jax
import jax.numpy as jnp
from jax import lax

TRUNC = 1279
NLAT = 2560
KP = 1281
PAIRS = 64
LEVELS = 32


def draw_points(key, part):
    key = jax.random.fold_in(key, 5)
    rows = jnp.arange(NLAT, dtype=jnp.int32)
    base = 20 + 4 * jnp.minimum(rows, NLAT - 1 - rows)
    reduce_by = 4 * jax.random.randint(key, (NLAT,), 0, 9, dtype=jnp.int32)
    middle = jnp.abs(2 * rows - (NLAT - 1)) <= 1
    reduce_by = jnp.where(middle, 0, reduce_by)
    return jnp.maximum(base - reduce_by, 20).astype(jnp.int32)


def draw_pair_low(key, part):
    key = jax.random.fold_in(key, 11)
    first_key, second_key = jax.random.split(key)
    half_count = (TRUNC + 1) // 2
    inner = jax.random.permutation(first_key, half_count - 2)[:PAIRS - 2] + 1
    ends = jnp.array([0, half_count - 1], dtype=jnp.int32)
    chosen = jnp.concatenate([ends, inner.astype(jnp.int32)])
    order = jax.random.permutation(second_key, PAIRS)
    return chosen[order].astype(jnp.int32)


def block_scale(own_key, extent, cuts, low, high):
    def one(position, parts):
        draws = jax.random.uniform(jax.random.fold_in(jax.random.fold_in(own_key, 6), position), (parts,), jnp.float32, low / len(cuts), high / len(cuts))
        return jnp.repeat(jnp.exp(draws), extent[position] // parts).reshape((-1,) + (1,) * (len(extent) - position - 1))

    level = one(*cuts[0])
    for cut in cuts[1:]:
        level = level * one(*cut)
    return level


def normal_values(key, shape, width, reach, cuts=(), kind=jnp.bfloat16):
    drawn = jax.random.normal(key, shape, jnp.float32) * width
    if len(cuts) > 0:
        drawn = block_scale(key, shape, cuts, -0.22, 0.18) * drawn
    return jnp.clip(drawn, min=-reach, max=reach).astype(kind)


def setup_inputs(seed: int = 0) -> dict:
    key_list = jax.random.split(jax.random.key(seed), 7)
    return {
        "fourier_in": normal_values(key_list[0], (2, LEVELS, NLAT, 4 * PAIRS), 1.0, 6.0, ((1, 8), (2, 64))),
        "table": normal_values(key_list[1], (PAIRS, KP, NLAT), NLAT ** -0.5, 0.125, ((0, 64), (2, 8))),
        "points": draw_points(jax.random.fold_in(key_list[6], 71), 0),
        "pair_low": draw_pair_low(jax.random.fold_in(key_list[6], 71), 0),
        "gamma": jnp.clip(jnp.exp(jax.random.uniform(key_list[4], (LEVELS,), jnp.float32, math.log(1.0), math.log(100.0))), 1.0, 100.0),
        "beta": jnp.clip(jax.random.uniform(key_list[5], (LEVELS,), jnp.float32, 0.5, 2.0), 0.5, 2.0),
    }


def solve_levels(spectra, gamma, beta, eig):
    drive = spectra[0]
    mass = spectra[1]
    gval = gamma[:, None, None]
    bval = beta[:, None, None]
    solved = (drive - bval * eig * mass) / (1.0 + gval * eig)
    return jnp.stack([solved, mass + bval * solved], axis=0).astype(jnp.bfloat16)


def reference(fourier_in, table, points, pair_low, gamma, beta):
    pts = points.astype(jnp.float32)
    weights = NLAT * pts / jnp.sum(pts)
    limit = jnp.minimum(TRUNC, points // 2 - 1)
    data = fourier_in.reshape(2, LEVELS, NLAT, PAIRS, 2, 2)
    data = jnp.transpose(data, (3, 0, 1, 4, 5, 2))
    kidx = jnp.arange(KP, dtype=jnp.int32)

    def one_pair(args):
        block, plane, low = args
        wnum = jnp.stack([low, TRUNC - low])
        keep = (wnum[:, None] <= limit[None, :])[:, None, :]
        weighted = jnp.where(keep, block.astype(jnp.float32) * weights, 0.0).astype(jnp.bfloat16)
        cols = weighted.reshape(-1, NLAT)
        raw = jnp.dot(cols, plane.T, preferred_element_type=jnp.float32).reshape(2, LEVELS, 2, 2, KP)
        first = kidx <= TRUNC - low
        spectra = jnp.where(first, raw[:, :, 0], raw[:, :, 1])
        degree = jnp.where(first, low + kidx, kidx - 1).astype(jnp.float32)
        eig = degree * (degree + 1.0) / (TRUNC * (TRUNC + 1.0))
        spec = solve_levels(spectra, gamma, beta, eig)
        zero = jnp.zeros_like(spec)
        expanded = jnp.stack([jnp.where(first, spec, zero), jnp.where(first, zero, spec)], axis=2)
        result = jnp.dot(expanded.reshape(-1, KP), plane, preferred_element_type=jnp.float32)
        result = result.reshape(2, LEVELS, 2, 2, NLAT)
        return jnp.where(keep, result, 0.0).astype(jnp.bfloat16)

    outs = lax.map(one_pair, (data, table, pair_low))
    outs = jnp.transpose(outs, (1, 2, 5, 0, 3, 4))
    return outs.reshape(2, LEVELS, NLAT, 4 * PAIRS)
```

```python
import jax
import jax.numpy as jnp
from jax import lax
from jax.experimental import pallas as pl
from jax.experimental.pallas import tpu as pltpu
from jax.sharding import PartitionSpec as P

F = 2
V = 4
R = 40
PAIRS = 64
SLABS = 8
SLAB = 320
KP = 1281
CUT = KP - 2
NLAT = 2560
STEPS = R // 4
COLS = 32
HALF = 640
NEAR = 8 * 10**9
NEARS = 4

NT = (((1,), (1,)), ((), ()))
NN = (((1,), (0,)), ((), ()))
TN = (((0,), (0,)), ((), ()))
VMEM = pl.BlockSpec(memory_space=pltpu.VMEM)
ANY = pl.BlockSpec(memory_space=pl.ANY)
SMEM = pl.BlockSpec(memory_space=pltpu.SMEM)


def iota(shape, dim):
    return lax.broadcasted_iota(jnp.int32, shape, dim)


def ones_where(cond):
    return jnp.where(cond, 1.0, 0.0).astype(jnp.bfloat16)


def mul(a, b, dims):
    return lax.dot_general(a, b, dims, preferred_element_type=jnp.float32)


def by_member():
    row = iota((4 * PAIRS, 4 * PAIRS), 0)
    return ones_where(iota((4 * PAIRS, 4 * PAIRS), 1) == 4 * (row & (PAIRS - 1)) + (row >> 6))


def by_place():
    lane = iota((1, STEPS * 128), 1)
    source = ((lane >> 3) & 1) * V + ((lane >> 1) & 3)
    source = source * R + 4 * (lane >> 7) + ((lane >> 5) & 3)
    return ones_where(iota((F * V * R, STEPS * 128), 0) == source)


def lane_part(shape):
    lane = iota(shape, 1)
    return ((lane >> 4) & 1) * 2 + (lane & 1)


def pack_kernel(x_ref, o_ref):
    x = x_ref[...].astype(jnp.float32).reshape(F * V * R, 4 * PAIRS).astype(jnp.bfloat16)
    turned = mul(by_member(), x, NT).astype(jnp.bfloat16)
    placed = mul(turned, by_place(), NN)
    part = lane_part((PAIRS, STEPS * 128))
    out = placed[:PAIRS]
    for q in range(1, 4):
        out = jnp.where(part == q, placed[q * PAIRS:(q + 1) * PAIRS], out)
    halves = jnp.stack([out[:, :HALF], out[:, HALF:]], axis=0)
    o_ref[...] = jnp.swapaxes(halves, 0, 1).astype(jnp.bfloat16)


def unpack_kernel(b_ref, o_ref):
    b = jnp.swapaxes(b_ref[...].astype(jnp.float32), 0, 1)
    b = jnp.concatenate([b[0], b[1]], axis=1)
    part = lane_part((PAIRS, STEPS * 128))
    parts = [jnp.where(part == q, b, 0.0).astype(jnp.bfloat16) for q in range(4)]
    turned = mul(by_place(), jnp.concatenate(parts, axis=0), NT).astype(jnp.bfloat16)
    x = mul(turned, by_member(), NN)
    o_ref[...] = x.reshape(F, V, R, 4 * PAIRS).astype(jnp.bfloat16)


def spread_rows():
    row = iota((STEPS * SLABS, SLAB), 0)
    gap = iota((STEPS * SLABS, SLAB), 1) - (row & 7) * R - 4 * (row >> 3)
    return ones_where((gap >= 0) & (gap < 4))


def own_group():
    return (iota((4 * COLS, SLAB), 0) >> 5) == (iota((4 * COLS, SLAB), 1) & 3)


def coef_kernel(low_ref, lev_ref, gamma_ref, beta_ref, points_ref, scale_ref, mask_ref, level_ref):
    low = low_ref[0]
    points = jnp.concatenate([points_ref[:, s * SLAB:(s + 1) * SLAB] for s in range(SLABS)], axis=0)
    pts = points.astype(jnp.float32)
    weights = NLAT * pts / jnp.sum(pts)
    limit = jnp.minimum(CUT, (points >> 1) - 1)
    rows = jnp.stack([jnp.where(low <= limit, weights, 0.0), jnp.where(CUT - low <= limit, weights, 0.0)], axis=0)
    for s in range(SLABS):
        scale_ref[s] = rows[:, s, :]
    columns = limit.astype(jnp.float32).T
    lane = iota((SLAB, 128), 1)
    group = (lane >> 5) == (iota((SLAB, 128), 0) & 3)
    wnum = jnp.where((lane & 16) == 0, low, CUT - low).astype(jnp.float32)
    for s in range(SLABS):
        mask_ref[s] = ones_where(group & (wnum <= columns[:, s:s + 1]))
    level = iota((SLABS, 128), 0) >> 1
    gval = jnp.zeros((SLABS, 128), jnp.float32)
    bval = jnp.zeros((SLABS, 128), jnp.float32)
    for v in range(V):
        gval = jnp.where(level == v, gamma_ref[lev_ref[0] * V + v], gval)
        bval = jnp.where(level == v, beta_ref[lev_ref[0] * V + v], bval)
    level_ref[0] = gval
    level_ref[1] = bval


def members(pair):
    return jnp.concatenate([jnp.broadcast_to(pair[m:m + 1], (COLS // 2, SLAB)) for m in range(2)], axis=0)


def weigh_kernel(y_ref, scale_ref, o_ref):
    spread = spread_rows()
    group = own_group()
    y = jnp.swapaxes(y_ref[...].astype(jnp.float32), 0, 1)
    for s in range(SLABS):
        rows = y[:, s * SLABS:(s + 1) * SLABS]
        block = jnp.concatenate([rows[j // 5, :, (j % 5) * 128:(j % 5 + 1) * 128] for j in range(STEPS)], axis=0)
        turned = jnp.where(group, mul(block.astype(jnp.bfloat16), spread, TN), 0.0)
        turned = turned[:32] + turned[32:64] + turned[64:96] + turned[96:]
        o_ref[s] = (turned * members(scale_ref[s])).astype(jnp.bfloat16)


def slab_order(lev):
    way = 2 - 4 * (lev & 1)
    behind, ahead, far = (lev - way) & 7, (lev + way) & 7, (lev + 4) & 7
    return [lev, lev ^ 1, behind, behind ^ 1, ahead ^ 1, ahead, far, far ^ 1]


def add_up(raw, w_ref, slabs, tabs):
    for slab, tab in zip(slabs, tabs):
        term = mul(w_ref[slab], tab[...], NN)
        raw = term if raw is None else raw + term
    return raw


def near_kernel(lev_ref, w_ref, *refs):
    tabs, raw_ref, kept_refs, sems = refs[:NEARS], refs[NEARS], refs[NEARS + 1:-1], refs[-1]
    copies = [pltpu.make_async_copy(tabs[n], kept_refs[n], sems.at[n]) for n in range(NEARS)]
    for copy in copies:
        copy.start()
    slabs = slab_order(lev_ref[0])
    raw = None
    for n in range(NEARS):
        copies[n].wait()
        raw = add_up(raw, w_ref, slabs[n:n + 1], [kept_refs[n]])
    raw_ref[...] = raw


def far_kernel(lev_ref, w_ref, raw_ref, *refs):
    *tabs, total_ref = refs
    total_ref[...] = add_up(raw_ref[...], w_ref, slab_order(lev_ref[0])[4:], tabs)


def pass_kernel(token_ref, tab_ref, same_ref):
    pass


def solve_kernel(low_ref, lev_ref, level_ref, w_ref, mask_ref, raw_ref, *refs):
    *tabs, o_ref, out_ref = refs
    low = low_ref[0]
    slabs = slab_order(lev_ref[0])
    wide = add_up(raw_ref[...], w_ref, slabs[7:], tabs[7:])
    kidx = iota((1, KP), 1)
    first = kidx <= CUT - low
    degree = jnp.where(first, low + kidx, kidx - 1).astype(jnp.float32)
    eig = degree * (degree + 1.0) / (CUT * (CUT + 1.0))
    gval = level_ref[0, :, 0:1]
    bval = level_ref[1, :, 0:1]
    spectra = jnp.where(first, wide[:16], wide[16:])
    drive, mass = spectra[:8], spectra[8:]
    solved = (drive - bval * eig * mass) / (1.0 + gval * eig)
    spec = jnp.concatenate([solved, mass + bval * solved], axis=0)
    expanded = [jnp.where(first, spec, 0.0), jnp.where(first, 0.0, spec)] * 4
    expanded = jnp.concatenate(expanded, axis=0).T.astype(jnp.bfloat16)
    spread = spread_rows()
    for slab, tab in zip(slabs, tabs):
        rows = mul(tab[:, :KP - 1], expanded[:KP - 1], NN)
        rows = rows + tab[:, KP - 1:].astype(jnp.float32) * expanded[KP - 1:].astype(jnp.float32)
        rows = rows.astype(jnp.bfloat16) * mask_ref[slab]
        block = mul(spread, rows, NN)
        place = pl.ds(pl.multiple_of(slab * SLABS, SLABS), SLABS)
        for j in range(STEPS):
            out_ref[j // 5, place, (j % 5) * 128:(j % 5 + 1) * 128] = block[j * SLABS:(j + 1) * SLABS]
    o_ref[...] = jnp.swapaxes(out_ref[...], 0, 1).astype(jnp.bfloat16)


def params(mib):
    return pltpu.CompilerParams(vmem_limit_bytes=mib * 1024 * 1024)


def cost(rows, depth, columns):
    return pl.CostEstimate(flops=2 * max(rows, 256) * depth * columns, transcendentals=0,
                           bytes_accessed=2 * depth * columns)


def chunks():
    return jax.ShapeDtypeStruct((PAIRS, 2, HALF), jnp.bfloat16)


def pack(x):
    return pl.pallas_call(pack_kernel, out_shape=chunks(), in_specs=[VMEM], out_specs=VMEM,
                          compiler_params=params(12), cost_estimate=cost(PAIRS * 4, SLAB, 2 * KP), name="pack")(x)


def unpack(b):
    return pl.pallas_call(unpack_kernel, out_shape=jax.ShapeDtypeStruct((F, V, R, 4 * PAIRS), jnp.bfloat16),
                          in_specs=[VMEM], out_specs=VMEM, compiler_params=params(12), cost_estimate=cost(SLAB, PAIRS * 4, 2 * KP),
                          name="unpack")(b)


def coef(low, lev, gamma, beta, points):
    return pl.pallas_call(
        coef_kernel, out_shape=(jax.ShapeDtypeStruct((SLABS, 2, SLAB), jnp.float32),
                                jax.ShapeDtypeStruct((SLABS, SLAB, 128), jnp.bfloat16),
                                jax.ShapeDtypeStruct((2, SLABS, 128), jnp.float32)),
        in_specs=[SMEM] * 4 + [VMEM], out_specs=(VMEM,) * 3, compiler_params=params(8),
        name="coef")(low, lev, gamma, beta, points)


def like(tab):
    return jax.ShapeDtypeStruct(tab.shape, tab.dtype)


def weigh(y, scale):
    return pl.pallas_call(
        weigh_kernel, out_shape=jax.ShapeDtypeStruct((SLABS, COLS, SLAB), jnp.bfloat16),
        in_specs=[VMEM, VMEM], out_specs=VMEM, compiler_params=params(8),
        cost_estimate=cost(SLABS * 128, SLAB, 128), name="weigh")(y, scale)


def pass_on(token, tab):
    return pl.pallas_call(pass_kernel, out_shape=like(tab), in_specs=[ANY, ANY], out_specs=ANY,
                          input_output_aliases={1: 0}, compiler_params=params(1), name="pass_on")(token, tab)


RAW = jax.ShapeDtypeStruct((COLS, KP), jnp.float32)


def near(lev, w, tabs):
    return pl.pallas_call(
        near_kernel, out_shape=(RAW,) + tuple(like(t) for t in tabs), in_specs=[SMEM, VMEM] + [ANY] * NEARS,
        out_specs=(VMEM,) * (1 + NEARS), scratch_shapes=[pltpu.SemaphoreType.DMA((NEARS,))],
        compiler_params=params(8), cost_estimate=pl.CostEstimate(flops=NEAR, bytes_accessed=0, transcendentals=0),
        name="near")(lev, w, *tabs)


def far(lev, w, raw, tabs):
    return pl.pallas_call(
        far_kernel, out_shape=RAW, in_specs=[SMEM] + [VMEM] * (2 + len(tabs)), out_specs=VMEM,
        compiler_params=params(8), cost_estimate=cost(COLS, 3 * SLAB, KP), name="far")(lev, w, raw, *tabs)


def solve(low, lev, level, w, mask, raw, tabs):
    return pl.pallas_call(
        solve_kernel, out_shape=chunks(), in_specs=[SMEM] * 2 + [VMEM] * (4 + len(tabs)), out_specs=VMEM,
        scratch_shapes=[pltpu.VMEM((2, PAIRS, HALF), jnp.float32)],
        compiler_params=params(12), cost_estimate=cost(COLS, 9 * SLAB, KP),
        name="solve")(low, lev, level, w, mask, raw, *tabs)


def along_x(array):
    return lax.ppermute(array, "lev", [(d, (d + 2 - 4 * (d % 2)) % SLABS) for d in range(SLABS)])


def other_core(array):
    return lax.ppermute(array, "lev", [(d, d ^ 1) for d in range(SLABS)])


def local(fourier_in, table, points, pair_low, gamma, beta):
    lev = lax.axis_index("lev").astype(jnp.int32).reshape(1)
    own = jnp.swapaxes(table, 1, 2)[0]
    twin = other_core(own)
    first = along_x(own)
    second = along_x(twin)
    sent = pack(fourier_in)
    moved = lax.all_to_all(sent, "wave", split_axis=0, concat_axis=0, tiled=True)
    first = pass_on(sent, first)
    third = along_x(first)
    second = pass_on(sent, second)
    cores = [other_core(first), other_core(second)]
    scale, mask, level = coef(pair_low, lev, gamma, beta, points.reshape(1, NLAT))
    weighted = weigh(moved, scale)
    raw, *tabs = near(lev, weighted, [own, twin, first, second])
    third = pass_on(raw, third)
    tabs += cores + [third]
    raw = far(lev, weighted, raw, tabs[NEARS:])
    tabs += [other_core(third)]
    result = solve(pair_low, lev, level, weighted, mask, raw, tabs)
    back = lax.all_to_all(result, "wave", split_axis=0, concat_axis=0, tiled=True)
    return unpack(back)


def solution(mesh):
    placed = (P(None, "lev", "wave", None), P("wave", None, "lev"), P(), P("wave"), P(), P())
    return jax.shard_map(
        local, mesh=mesh, in_specs=placed, out_specs=P(None, "lev", "wave", None), check_vma=False
    )
```

```python
import jax
import jax.numpy as jnp
from jax import lax
from jax.experimental import pallas as pl
from jax.experimental.pallas import tpu as pltpu
from jax.sharding import PartitionSpec as P

F = 2
V = 4
R = 40
PAIRS = 64
SLABS = 8
SLAB = 320
KP = 1281
CUT = KP - 2
NLAT = 2560
STEPS = R // 4
COLS = 32
HALF = 640
NEAR = 8 * 10**9
NEARS = 4

NT = (((1,), (1,)), ((), ()))
NN = (((1,), (0,)), ((), ()))
TN = (((0,), (0,)), ((), ()))
VMEM = pl.BlockSpec(memory_space=pltpu.VMEM)
ANY = pl.BlockSpec(memory_space=pl.ANY)
SMEM = pl.BlockSpec(memory_space=pltpu.SMEM)


def iota(shape, dim):
    return lax.broadcasted_iota(jnp.int32, shape, dim)


def ones_where(cond):
    return jnp.where(cond, 1.0, 0.0).astype(jnp.bfloat16)


def mul(a, b, dims):
    return lax.dot_general(a, b, dims, preferred_element_type=jnp.float32)


def by_member():
    row = iota((4 * PAIRS, 4 * PAIRS), 0)
    return ones_where(iota((4 * PAIRS, 4 * PAIRS), 1) == 4 * (row & (PAIRS - 1)) + (row >> 6))


def by_place():
    lane = iota((1, STEPS * 128), 1)
    source = ((lane >> 3) & 1) * V + ((lane >> 1) & 3)
    source = source * R + 4 * (lane >> 7) + ((lane >> 5) & 3)
    return ones_where(iota((F * V * R, STEPS * 128), 0) == source)


def lane_part(shape):
    lane = iota(shape, 1)
    return ((lane >> 4) & 1) * 2 + (lane & 1)


def pack_kernel(x_ref, o_ref):
    x = x_ref[...].astype(jnp.float32).reshape(F * V * R, 4 * PAIRS).astype(jnp.bfloat16)
    turned = mul(by_member(), x, NT).astype(jnp.bfloat16)
    placed = mul(turned, by_place(), NN)
    part = lane_part((PAIRS, STEPS * 128))
    out = placed[:PAIRS]
    for q in range(1, 4):
        out = jnp.where(part == q, placed[q * PAIRS:(q + 1) * PAIRS], out)
    halves = jnp.stack([out[:, :HALF], out[:, HALF:]], axis=0)
    o_ref[...] = jnp.swapaxes(halves, 0, 1).astype(jnp.bfloat16)


def unpack_kernel(b_ref, o_ref):
    b = jnp.swapaxes(b_ref[...].astype(jnp.float32), 0, 1)
    b = jnp.concatenate([b[0], b[1]], axis=1)
    part = lane_part((PAIRS, STEPS * 128))
    parts = [jnp.where(part == q, b, 0.0).astype(jnp.bfloat16) for q in range(4)]
    turned = mul(by_place(), jnp.concatenate(parts, axis=0), NT).astype(jnp.bfloat16)
    x = mul(turned, by_member(), NN)
    o_ref[...] = x.reshape(F, V, R, 4 * PAIRS).astype(jnp.bfloat16)


def spread_rows():
    row = iota((STEPS * SLABS, SLAB), 0)
    gap = iota((STEPS * SLABS, SLAB), 1) - (row & 7) * R - 4 * (row >> 3)
    return ones_where((gap >= 0) & (gap < 4))


def own_group():
    return (iota((4 * COLS, SLAB), 0) >> 5) == (iota((4 * COLS, SLAB), 1) & 3)


def coef_kernel(low_ref, lev_ref, gamma_ref, beta_ref, points_ref, scale_ref, level_ref):
    low = low_ref[0]
    points = jnp.concatenate([points_ref[:, s * SLAB:(s + 1) * SLAB] for s in range(SLABS)], axis=0)
    pts = points.astype(jnp.float32)
    weights = NLAT * pts / jnp.sum(pts)
    limit = jnp.minimum(CUT, (points >> 1) - 1)
    rows = jnp.stack([jnp.where(low <= limit, weights, 0.0), jnp.where(CUT - low <= limit, weights, 0.0)], axis=0)
    for s in range(SLABS):
        scale_ref[s] = rows[:, s, :]
    level = iota((SLABS, 128), 0) >> 1
    gval = jnp.zeros((SLABS, 128), jnp.float32)
    bval = jnp.zeros((SLABS, 128), jnp.float32)
    for v in range(V):
        gval = jnp.where(level == v, gamma_ref[lev_ref[0] * V + v], gval)
        bval = jnp.where(level == v, beta_ref[lev_ref[0] * V + v], bval)
    level_ref[0] = gval
    level_ref[1] = bval


def members(pair):
    return jnp.concatenate([jnp.broadcast_to(pair[m:m + 1], (COLS // 2, SLAB)) for m in range(2)], axis=0)


def weigh_kernel(y_ref, scale_ref, o_ref):
    spread = spread_rows()
    group = own_group()
    y = jnp.swapaxes(y_ref[...].astype(jnp.float32), 0, 1)
    for s in range(SLABS):
        rows = y[:, s * SLABS:(s + 1) * SLABS]
        block = jnp.concatenate([rows[j // 5, :, (j % 5) * 128:(j % 5 + 1) * 128] for j in range(STEPS)], axis=0)
        turned = jnp.where(group, mul(block.astype(jnp.bfloat16), spread, TN), 0.0)
        turned = turned[:32] + turned[32:64] + turned[64:96] + turned[96:]
        o_ref[s] = (turned * members(scale_ref[s])).astype(jnp.bfloat16)


def slab_order(lev):
    way = 2 - 4 * (lev & 1)
    behind, ahead, far = (lev - way) & 7, (lev + way) & 7, (lev + 4) & 7
    return [lev, lev ^ 1, behind, behind ^ 1, ahead ^ 1, ahead, far, far ^ 1]


def add_up(raw, w_ref, slabs, tabs):
    for slab, tab in zip(slabs, tabs):
        term = mul(w_ref[slab], tab[...], NN)
        raw = term if raw is None else raw + term
    return raw


def near_kernel(lev_ref, w_ref, *refs):
    tabs, raw_ref, kept_refs, sems = refs[:NEARS], refs[NEARS], refs[NEARS + 1:-1], refs[-1]
    copies = [pltpu.make_async_copy(tabs[n], kept_refs[n], sems.at[n]) for n in range(NEARS)]
    for copy in copies:
        copy.start()
    slabs = slab_order(lev_ref[0])
    raw = None
    for n in range(NEARS):
        copies[n].wait()
        raw = add_up(raw, w_ref, slabs[n:n + 1], [kept_refs[n]])
    raw_ref[...] = raw


def far_kernel(lev_ref, w_ref, raw_ref, *refs):
    *tabs, total_ref = refs
    total_ref[...] = add_up(raw_ref[...], w_ref, slab_order(lev_ref[0])[4:], tabs)


def pass_kernel(token_ref, tab_ref, same_ref):
    pass


def solve_kernel(low_ref, lev_ref, level_ref, w_ref, scale_ref, raw_ref, *refs):
    *tabs, o_ref, out_ref = refs
    low = low_ref[0]
    slabs = slab_order(lev_ref[0])
    wide = add_up(raw_ref[...], w_ref, slabs[7:], tabs[7:])
    kidx = iota((1, KP), 1)
    first = kidx <= CUT - low
    degree = jnp.where(first, low + kidx, kidx - 1).astype(jnp.float32)
    eig = degree * (degree + 1.0) / (CUT * (CUT + 1.0))
    gval = level_ref[0, :, 0:1]
    bval = level_ref[1, :, 0:1]
    spectra = jnp.where(first, wide[:16], wide[16:])
    drive, mass = spectra[:8], spectra[8:]
    solved = (drive - bval * eig * mass) / (1.0 + gval * eig)
    spec = jnp.concatenate([solved, mass + bval * solved], axis=0)
    expanded = jnp.concatenate([jnp.where(first, spec, 0.0), jnp.where(first, 0.0, spec)], axis=0).astype(jnp.bfloat16)
    spread = spread_rows()
    group = own_group()
    for slab, tab in zip(slabs, tabs):
        rows = jnp.where(members(scale_ref[slab]) > 0.0, mul(expanded, tab[...], NT), 0.0)
        rows = jnp.where(group, jnp.concatenate([rows] * 4, axis=0), 0.0).astype(jnp.bfloat16)
        block = mul(spread, rows, NT)
        place = pl.ds(pl.multiple_of(slab * SLABS, SLABS), SLABS)
        for j in range(STEPS):
            out_ref[j // 5, place, (j % 5) * 128:(j % 5 + 1) * 128] = block[j * SLABS:(j + 1) * SLABS]
    o_ref[...] = jnp.swapaxes(out_ref[...], 0, 1).astype(jnp.bfloat16)


def params(mib):
    return pltpu.CompilerParams(vmem_limit_bytes=mib * 1024 * 1024)


def cost(rows, depth, columns):
    return pl.CostEstimate(flops=2 * max(rows, 256) * depth * columns, transcendentals=0,
                           bytes_accessed=2 * depth * columns)


def chunks():
    return jax.ShapeDtypeStruct((PAIRS, 2, HALF), jnp.bfloat16)


def pack(x):
    return pl.pallas_call(pack_kernel, out_shape=chunks(), in_specs=[VMEM], out_specs=VMEM,
                          compiler_params=params(12), cost_estimate=cost(PAIRS * 4, SLAB, 2 * KP), name="pack")(x)


def unpack(b):
    return pl.pallas_call(unpack_kernel, out_shape=jax.ShapeDtypeStruct((F, V, R, 4 * PAIRS), jnp.bfloat16),
                          in_specs=[VMEM], out_specs=VMEM, compiler_params=params(12), cost_estimate=cost(SLAB, PAIRS * 4, 2 * KP),
                          name="unpack")(b)


def coef(low, lev, gamma, beta, points):
    return pl.pallas_call(
        coef_kernel, out_shape=(jax.ShapeDtypeStruct((SLABS, 2, SLAB), jnp.float32),
                                jax.ShapeDtypeStruct((2, SLABS, 128), jnp.float32)),
        in_specs=[SMEM] * 4 + [VMEM], out_specs=(VMEM,) * 2, compiler_params=params(8),
        name="coef")(low, lev, gamma, beta, points)


def like(tab):
    return jax.ShapeDtypeStruct(tab.shape, tab.dtype)


def weigh(y, scale):
    return pl.pallas_call(
        weigh_kernel, out_shape=jax.ShapeDtypeStruct((SLABS, COLS, SLAB), jnp.bfloat16),
        in_specs=[VMEM, VMEM], out_specs=VMEM, compiler_params=params(8),
        cost_estimate=cost(SLABS * 128, SLAB, 128), name="weigh")(y, scale)


def pass_on(token, tab):
    return pl.pallas_call(pass_kernel, out_shape=like(tab), in_specs=[ANY, ANY], out_specs=ANY,
                          input_output_aliases={1: 0}, compiler_params=params(1), name="pass_on")(token, tab)


RAW = jax.ShapeDtypeStruct((COLS, KP), jnp.float32)


def near(lev, w, tabs):
    return pl.pallas_call(
        near_kernel, out_shape=(RAW,) + tuple(like(t) for t in tabs), in_specs=[SMEM, VMEM] + [ANY] * NEARS,
        out_specs=(VMEM,) * (1 + NEARS), scratch_shapes=[pltpu.SemaphoreType.DMA((NEARS,))],
        compiler_params=params(8), cost_estimate=pl.CostEstimate(flops=NEAR, bytes_accessed=0, transcendentals=0),
        name="near")(lev, w, *tabs)


def far(lev, w, raw, tabs):
    return pl.pallas_call(
        far_kernel, out_shape=RAW, in_specs=[SMEM] + [VMEM] * (2 + len(tabs)), out_specs=VMEM,
        compiler_params=params(8), cost_estimate=cost(COLS, 3 * SLAB, KP), name="far")(lev, w, raw, *tabs)


def solve(low, lev, level, w, scale, raw, tabs):
    return pl.pallas_call(
        solve_kernel, out_shape=chunks(), in_specs=[SMEM] * 2 + [VMEM] * (4 + len(tabs)), out_specs=VMEM,
        scratch_shapes=[pltpu.VMEM((2, PAIRS, HALF), jnp.float32)],
        compiler_params=params(12), cost_estimate=cost(COLS, 9 * SLAB, KP),
        name="solve")(low, lev, level, w, scale, raw, *tabs)


def along_x(array):
    return lax.ppermute(array, "lev", [(d, (d + 2 - 4 * (d % 2)) % SLABS) for d in range(SLABS)])


def other_core(array):
    return lax.ppermute(array, "lev", [(d, d ^ 1) for d in range(SLABS)])


def local(fourier_in, table, points, pair_low, gamma, beta):
    lev = lax.axis_index("lev").astype(jnp.int32).reshape(1)
    own = jnp.swapaxes(table, 1, 2)[0]
    twin = other_core(own)
    first = along_x(own)
    second = along_x(twin)
    sent = pack(fourier_in)
    moved = lax.all_to_all(sent, "wave", split_axis=0, concat_axis=0, tiled=True)
    first = pass_on(sent, first)
    third = along_x(first)
    second = pass_on(sent, second)
    cores = [other_core(first), other_core(second)]
    scale, level = coef(pair_low, lev, gamma, beta, points.reshape(1, NLAT))
    weighted = weigh(moved, scale)
    raw, *tabs = near(lev, weighted, [own, twin, first, second])
    third = pass_on(raw, third)
    tabs += cores + [third]
    raw = far(lev, weighted, raw, tabs[NEARS:])
    tabs += [other_core(third)]
    result = solve(pair_low, lev, level, weighted, scale, raw, tabs)
    back = lax.all_to_all(result, "wave", split_axis=0, concat_axis=0, tiled=True)
    return unpack(back)


def solution(mesh):
    placed = (P(None, "lev", "wave", None), P("wave", None, "lev"), P(), P("wave"), P(), P())
    return jax.shard_map(
        local, mesh=mesh, in_specs=placed, out_specs=P(None, "lev", "wave", None), check_vma=False
    )
```

```python
import jax
import jax.numpy as jnp
from jax import lax
from jax.experimental import pallas as pl
from jax.experimental.pallas import tpu as pltpu
from jax.sharding import PartitionSpec as P

F = 2
V = 4
R = 40
PAIRS = 64
SLABS = 8
SLAB = 320
KP = 1281
CUT = KP - 2
NLAT = 2560
STEPS = R // 4
COLS = 32
HALF = 640
NEAR = 8 * 10**9
NEARS = 4
FARS = 3

NT = (((1,), (1,)), ((), ()))
NN = (((1,), (0,)), ((), ()))
TN = (((0,), (0,)), ((), ()))
VMEM = pl.BlockSpec(memory_space=pltpu.VMEM)
ANY = pl.BlockSpec(memory_space=pl.ANY)
SMEM = pl.BlockSpec(memory_space=pltpu.SMEM)


def iota(shape, dim):
    return lax.broadcasted_iota(jnp.int32, shape, dim)


def ones_where(cond):
    return jnp.where(cond, 1.0, 0.0).astype(jnp.bfloat16)


def mul(a, b, dims):
    return lax.dot_general(a, b, dims, preferred_element_type=jnp.float32)


def by_member():
    row = iota((4 * PAIRS, 4 * PAIRS), 0)
    return ones_where(iota((4 * PAIRS, 4 * PAIRS), 1) == 4 * (row & (PAIRS - 1)) + (row >> 6))


def by_place():
    lane = iota((1, STEPS * 128), 1)
    source = ((lane >> 3) & 1) * V + ((lane >> 1) & 3)
    source = source * R + 4 * (lane >> 7) + ((lane >> 5) & 3)
    return ones_where(iota((F * V * R, STEPS * 128), 0) == source)


def lane_part(shape):
    lane = iota(shape, 1)
    return ((lane >> 4) & 1) * 2 + (lane & 1)


def pack_kernel(x_ref, o_ref):
    x = x_ref[...].astype(jnp.float32).reshape(F * V * R, 4 * PAIRS).astype(jnp.bfloat16)
    turned = mul(by_member(), x, NT).astype(jnp.bfloat16)
    placed = mul(turned, by_place(), NN)
    part = lane_part((PAIRS, STEPS * 128))
    out = placed[:PAIRS]
    for q in range(1, 4):
        out = jnp.where(part == q, placed[q * PAIRS:(q + 1) * PAIRS], out)
    halves = jnp.stack([out[:, :HALF], out[:, HALF:]], axis=0)
    o_ref[...] = jnp.swapaxes(halves, 0, 1).astype(jnp.bfloat16)


def unpack_kernel(b_ref, o_ref):
    b = jnp.swapaxes(b_ref[...].astype(jnp.float32), 0, 1)
    b = jnp.concatenate([b[0], b[1]], axis=1)
    part = lane_part((PAIRS, STEPS * 128))
    parts = [jnp.where(part == q, b, 0.0).astype(jnp.bfloat16) for q in range(4)]
    turned = mul(by_place(), jnp.concatenate(parts, axis=0), NT).astype(jnp.bfloat16)
    x = mul(turned, by_member(), NN)
    o_ref[...] = x.reshape(F, V, R, 4 * PAIRS).astype(jnp.bfloat16)


def spread_rows():
    row = iota((STEPS * SLABS, SLAB), 0)
    gap = iota((STEPS * SLABS, SLAB), 1) - (row & 7) * R - 4 * (row >> 3)
    return ones_where((gap >= 0) & (gap < 4))


def own_group():
    return (iota((4 * COLS, SLAB), 0) >> 5) == (iota((4 * COLS, SLAB), 1) & 3)


def coef_kernel(low_ref, lev_ref, gamma_ref, beta_ref, points_ref, scale_ref, level_ref):
    low = low_ref[0]
    points = jnp.concatenate([points_ref[:, s * SLAB:(s + 1) * SLAB] for s in range(SLABS)], axis=0)
    pts = points.astype(jnp.float32)
    weights = NLAT * pts / jnp.sum(pts)
    limit = jnp.minimum(CUT, (points >> 1) - 1)
    rows = jnp.stack([jnp.where(low <= limit, weights, 0.0), jnp.where(CUT - low <= limit, weights, 0.0)], axis=0)
    for s in range(SLABS):
        scale_ref[s] = rows[:, s, :]
    level = iota((SLABS, 128), 0) >> 1
    gval = jnp.zeros((SLABS, 128), jnp.float32)
    bval = jnp.zeros((SLABS, 128), jnp.float32)
    for v in range(V):
        gval = jnp.where(level == v, gamma_ref[lev_ref[0] * V + v], gval)
        bval = jnp.where(level == v, beta_ref[lev_ref[0] * V + v], bval)
    level_ref[0] = gval
    level_ref[1] = bval


def members(pair):
    return jnp.concatenate([jnp.broadcast_to(pair[m:m + 1], (COLS // 2, SLAB)) for m in range(2)], axis=0)


def weigh_kernel(y_ref, scale_ref, o_ref):
    spread = spread_rows()
    group = own_group()
    y = jnp.swapaxes(y_ref[...].astype(jnp.float32), 0, 1)
    for s in range(SLABS):
        rows = y[:, s * SLABS:(s + 1) * SLABS]
        block = jnp.concatenate([rows[j // 5, :, (j % 5) * 128:(j % 5 + 1) * 128] for j in range(STEPS)], axis=0)
        turned = jnp.where(group, mul(block.astype(jnp.bfloat16), spread, TN), 0.0)
        turned = turned[:32] + turned[32:64] + turned[64:96] + turned[96:]
        o_ref[s] = (turned * members(scale_ref[s])).astype(jnp.bfloat16)


def slab_order(lev):
    way = 2 - 4 * (lev & 1)
    behind, ahead, far = (lev - way) & 7, (lev + way) & 7, (lev + 4) & 7
    return [lev, lev ^ 1, behind, behind ^ 1, ahead ^ 1, ahead, far, far ^ 1]


def add_up(raw, w_ref, slabs, tabs):
    for slab, tab in zip(slabs, tabs):
        term = mul(w_ref[slab], tab[...], NN)
        raw = term if raw is None else raw + term
    return raw


def near_kernel(lev_ref, w_ref, *refs):
    tabs, raw_ref, turned, held, sems = refs[:NEARS], refs[NEARS], refs[NEARS + 1:2 * NEARS + 1], refs[-2], refs[-1]
    copies = [pltpu.make_async_copy(tabs[n], held.at[n], sems.at[n]) for n in range(NEARS)]
    for copy in copies:
        copy.start()
    slabs = slab_order(lev_ref[0])
    raw = None
    for n in range(NEARS):
        copies[n].wait()
        raw = add_up(raw, w_ref, slabs[n:n + 1], [held.at[n]])
        turned[n][...] = held[n].T
    raw_ref[...] = raw


def far_kernel(lev_ref, w_ref, raw_ref, *refs):
    tabs, total_ref, turned = refs[:FARS], refs[FARS], refs[FARS + 1:]
    total_ref[...] = add_up(raw_ref[...], w_ref, slab_order(lev_ref[0])[NEARS:], tabs)
    for tab, turn in zip(tabs, turned):
        turn[...] = tab[...].T


def pass_kernel(token_ref, tab_ref, same_ref):
    pass


def solve_kernel(low_ref, lev_ref, level_ref, w_ref, scale_ref, raw_ref, *refs):
    *tabs, o_ref, out_ref = refs
    low = low_ref[0]
    slabs = slab_order(lev_ref[0])
    wide = add_up(raw_ref[...], w_ref, slabs[7:], tabs[7:])
    kidx = iota((1, KP), 1)
    first = kidx <= CUT - low
    degree = jnp.where(first, low + kidx, kidx - 1).astype(jnp.float32)
    eig = degree * (degree + 1.0) / (CUT * (CUT + 1.0))
    gval = level_ref[0, :, 0:1]
    bval = level_ref[1, :, 0:1]
    spectra = jnp.where(first, wide[:16], wide[16:])
    drive, mass = spectra[:8], spectra[8:]
    solved = (drive - bval * eig * mass) / (1.0 + gval * eig)
    spec = jnp.concatenate([solved, mass + bval * solved], axis=0)
    expanded = jnp.concatenate([jnp.where(first, spec, 0.0), jnp.where(first, 0.0, spec)], axis=0).astype(jnp.bfloat16)
    spread = spread_rows()
    group = own_group()
    for n, slab in enumerate(slabs):
        rows = mul(expanded, tabs[n][...], NN if n < NEARS + FARS else NT)
        rows = jnp.where(members(scale_ref[slab]) > 0.0, rows, 0.0)
        rows = jnp.where(group, jnp.concatenate([rows] * 4, axis=0), 0.0).astype(jnp.bfloat16)
        block = mul(spread, rows, NT)
        place = pl.ds(pl.multiple_of(slab * SLABS, SLABS), SLABS)
        for j in range(STEPS):
            out_ref[j // 5, place, (j % 5) * 128:(j % 5 + 1) * 128] = block[j * SLABS:(j + 1) * SLABS]
    o_ref[...] = jnp.swapaxes(out_ref[...], 0, 1).astype(jnp.bfloat16)


def params(mib):
    return pltpu.CompilerParams(vmem_limit_bytes=mib * 1024 * 1024)


def cost(rows, depth, columns):
    return pl.CostEstimate(flops=2 * max(rows, 256) * depth * columns, transcendentals=0,
                           bytes_accessed=2 * depth * columns)


def chunks():
    return jax.ShapeDtypeStruct((PAIRS, 2, HALF), jnp.bfloat16)


def pack(x):
    return pl.pallas_call(pack_kernel, out_shape=chunks(), in_specs=[VMEM], out_specs=VMEM,
                          compiler_params=params(12), cost_estimate=cost(PAIRS * 4, SLAB, 2 * KP), name="pack")(x)


def unpack(b):
    return pl.pallas_call(unpack_kernel, out_shape=jax.ShapeDtypeStruct((F, V, R, 4 * PAIRS), jnp.bfloat16),
                          in_specs=[VMEM], out_specs=VMEM, compiler_params=params(12), cost_estimate=cost(SLAB, PAIRS * 4, 2 * KP),
                          name="unpack")(b)


def coef(low, lev, gamma, beta, points):
    return pl.pallas_call(
        coef_kernel, out_shape=(jax.ShapeDtypeStruct((SLABS, 2, SLAB), jnp.float32),
                                jax.ShapeDtypeStruct((2, SLABS, 128), jnp.float32)),
        in_specs=[SMEM] * 4 + [VMEM], out_specs=(VMEM,) * 2, compiler_params=params(8),
        name="coef")(low, lev, gamma, beta, points)


def like(tab):
    return jax.ShapeDtypeStruct(tab.shape, tab.dtype)


def weigh(y, scale):
    return pl.pallas_call(
        weigh_kernel, out_shape=jax.ShapeDtypeStruct((SLABS, COLS, SLAB), jnp.bfloat16),
        in_specs=[VMEM, VMEM], out_specs=VMEM, compiler_params=params(8),
        cost_estimate=cost(SLABS * 128, SLAB, 128), name="weigh")(y, scale)


def pass_on(token, tab):
    return pl.pallas_call(pass_kernel, out_shape=like(tab), in_specs=[ANY, ANY], out_specs=ANY,
                          input_output_aliases={1: 0}, compiler_params=params(1), name="pass_on")(token, tab)


RAW = jax.ShapeDtypeStruct((COLS, KP), jnp.float32)


TURNED = jax.ShapeDtypeStruct((KP, SLAB), jnp.bfloat16)


def near(lev, w, tabs):
    return pl.pallas_call(
        near_kernel, out_shape=(RAW,) + (TURNED,) * NEARS, in_specs=[SMEM, VMEM] + [ANY] * NEARS,
        out_specs=(VMEM,) * (1 + NEARS),
        scratch_shapes=[pltpu.VMEM((NEARS, SLAB, KP), jnp.bfloat16), pltpu.SemaphoreType.DMA((NEARS,))],
        compiler_params=params(12), cost_estimate=pl.CostEstimate(flops=NEAR, bytes_accessed=0, transcendentals=0),
        name="near")(lev, w, *tabs)


def far(lev, w, raw, tabs):
    return pl.pallas_call(
        far_kernel, out_shape=(RAW,) + (TURNED,) * FARS, in_specs=[SMEM] + [VMEM] * (2 + FARS),
        out_specs=(VMEM,) * (1 + FARS),
        compiler_params=params(8), cost_estimate=cost(COLS, 3 * SLAB, KP), name="far")(lev, w, raw, *tabs)


def solve(low, lev, level, w, scale, raw, tabs):
    return pl.pallas_call(
        solve_kernel, out_shape=chunks(), in_specs=[SMEM] * 2 + [VMEM] * (4 + len(tabs)), out_specs=VMEM,
        scratch_shapes=[pltpu.VMEM((2, PAIRS, HALF), jnp.float32)],
        compiler_params=params(12), cost_estimate=cost(COLS, 9 * SLAB, KP),
        name="solve")(low, lev, level, w, scale, raw, *tabs)


def along_x(array):
    return lax.ppermute(array, "lev", [(d, (d + 2 - 4 * (d % 2)) % SLABS) for d in range(SLABS)])


def other_core(array):
    return lax.ppermute(array, "lev", [(d, d ^ 1) for d in range(SLABS)])


def local(fourier_in, table, points, pair_low, gamma, beta):
    lev = lax.axis_index("lev").astype(jnp.int32).reshape(1)
    own = jnp.swapaxes(table, 1, 2)[0]
    twin = other_core(own)
    first = along_x(own)
    second = along_x(twin)
    sent = pack(fourier_in)
    moved = lax.all_to_all(sent, "wave", split_axis=0, concat_axis=0, tiled=True)
    first = pass_on(sent, first)
    third = along_x(first)
    second = pass_on(sent, second)
    cores = [other_core(first), other_core(second)]
    scale, level = coef(pair_low, lev, gamma, beta, points.reshape(1, NLAT))
    weighted = weigh(moved, scale)
    raw, *tabs = near(lev, weighted, [own, twin, first, second])
    third = pass_on(raw, third)
    last = other_core(third)
    raw, *more = far(lev, weighted, raw, cores + [third])
    tabs += more + [last]
    result = solve(pair_low, lev, level, weighted, scale, raw, tabs)
    back = lax.all_to_all(result, "wave", split_axis=0, concat_axis=0, tiled=True)
    return unpack(back)


def solution(mesh):
    placed = (P(None, "lev", "wave", None), P("wave", None, "lev"), P(), P("wave"), P(), P())
    return jax.shard_map(
        local, mesh=mesh, in_specs=placed, out_specs=P(None, "lev", "wave", None), check_vma=False
    )
```

```python
import jax
import jax.numpy as jnp
from jax import lax
from jax.experimental import pallas as pl
from jax.experimental.pallas import tpu as pltpu
from jax.sharding import PartitionSpec as P

F = 2
V = 4
R = 40
PAIRS = 64
SLABS = 8
SLAB = 320
KP = 1281
CUT = KP - 2
NLAT = 2560
STEPS = R // 4
COLS = 32
HALF = 640
NEAR = 73 * 10**8
NEARS = 3
FARS = 4

NT = (((1,), (1,)), ((), ()))
NN = (((1,), (0,)), ((), ()))
TN = (((0,), (0,)), ((), ()))
VMEM = pl.BlockSpec(memory_space=pltpu.VMEM)
ANY = pl.BlockSpec(memory_space=pl.ANY)
SMEM = pl.BlockSpec(memory_space=pltpu.SMEM)


def iota(shape, dim):
    return lax.broadcasted_iota(jnp.int32, shape, dim)


def ones_where(cond):
    return jnp.where(cond, 1.0, 0.0).astype(jnp.bfloat16)


def mul(a, b, dims):
    return lax.dot_general(a, b, dims, preferred_element_type=jnp.float32)


def by_member():
    row = iota((4 * PAIRS, 4 * PAIRS), 0)
    return ones_where(iota((4 * PAIRS, 4 * PAIRS), 1) == 4 * (row & (PAIRS - 1)) + (row >> 6))


def by_place():
    lane = iota((1, STEPS * 128), 1)
    source = ((lane >> 3) & 1) * V + ((lane >> 1) & 3)
    source = source * R + 4 * (lane >> 7) + ((lane >> 5) & 3)
    return ones_where(iota((F * V * R, STEPS * 128), 0) == source)


def lane_part(shape):
    lane = iota(shape, 1)
    return ((lane >> 4) & 1) * 2 + (lane & 1)


def pack_kernel(x_ref, tab_ref, o_ref, copy_ref, held_x, held_tab, sems):
    get_x = pltpu.make_async_copy(x_ref, held_x, sems.at[0])
    get_tab = pltpu.make_async_copy(tab_ref, held_tab, sems.at[1])
    put_tab = pltpu.make_async_copy(held_tab, copy_ref, sems.at[2])
    get_x.start()
    get_tab.start()
    get_x.wait()
    x = held_x[...].astype(jnp.float32).reshape(F * V * R, 4 * PAIRS).astype(jnp.bfloat16)
    turned = mul(by_member(), x, NT).astype(jnp.bfloat16)
    get_tab.wait()
    put_tab.start()
    placed = mul(turned, by_place(), NN)
    part = lane_part((PAIRS, STEPS * 128))
    out = placed[:PAIRS]
    for q in range(1, 4):
        out = jnp.where(part == q, placed[q * PAIRS:(q + 1) * PAIRS], out)
    halves = jnp.stack([out[:, :HALF], out[:, HALF:]], axis=0)
    o_ref[...] = jnp.swapaxes(halves, 0, 1).astype(jnp.bfloat16)
    put_tab.wait()


def unpack_kernel(b_ref, o_ref):
    b = jnp.swapaxes(b_ref[...].astype(jnp.float32), 0, 1)
    b = jnp.concatenate([b[0], b[1]], axis=1)
    part = lane_part((PAIRS, STEPS * 128))
    parts = [jnp.where(part == q, b, 0.0).astype(jnp.bfloat16) for q in range(4)]
    turned = mul(by_place(), jnp.concatenate(parts, axis=0), NT).astype(jnp.bfloat16)
    x = mul(turned, by_member(), NN)
    o_ref[...] = x.reshape(F, V, R, 4 * PAIRS).astype(jnp.bfloat16)


def spread_rows():
    row = iota((STEPS * SLABS, SLAB), 0)
    gap = iota((STEPS * SLABS, SLAB), 1) - (row & 7) * R - 4 * (row >> 3)
    return ones_where((gap >= 0) & (gap < 4))


def own_group():
    return (iota((4 * COLS, SLAB), 0) >> 5) == (iota((4 * COLS, SLAB), 1) & 3)


def coef_kernel(low_ref, lev_ref, gamma_ref, beta_ref, points_ref, scale_ref, level_ref):
    low = low_ref[0]
    points = jnp.concatenate([points_ref[:, s * SLAB:(s + 1) * SLAB] for s in range(SLABS)], axis=0)
    pts = points.astype(jnp.float32)
    weights = NLAT * pts / jnp.sum(pts)
    limit = jnp.minimum(CUT, (points >> 1) - 1)
    rows = jnp.stack([jnp.where(low <= limit, weights, 0.0), jnp.where(CUT - low <= limit, weights, 0.0)], axis=0)
    for s in range(SLABS):
        scale_ref[s] = rows[:, s, :]
    level = iota((SLABS, 128), 0) >> 1
    gval = jnp.zeros((SLABS, 128), jnp.float32)
    bval = jnp.zeros((SLABS, 128), jnp.float32)
    for v in range(V):
        gval = jnp.where(level == v, gamma_ref[lev_ref[0] * V + v], gval)
        bval = jnp.where(level == v, beta_ref[lev_ref[0] * V + v], bval)
    level_ref[0] = gval
    level_ref[1] = bval


def members(pair):
    return jnp.concatenate([jnp.broadcast_to(pair[m:m + 1], (COLS // 2, SLAB)) for m in range(2)], axis=0)


def weigh_kernel(y_ref, scale_ref, o_ref):
    spread = spread_rows()
    group = own_group()
    y = jnp.swapaxes(y_ref[...].astype(jnp.float32), 0, 1)
    for s in range(SLABS):
        rows = y[:, s * SLABS:(s + 1) * SLABS]
        block = jnp.concatenate([rows[j // 5, :, (j % 5) * 128:(j % 5 + 1) * 128] for j in range(STEPS)], axis=0)
        turned = jnp.where(group, mul(block.astype(jnp.bfloat16), spread, TN), 0.0)
        turned = turned[:32] + turned[32:64] + turned[64:96] + turned[96:]
        o_ref[s] = (turned * members(scale_ref[s])).astype(jnp.bfloat16)


def slab_order(lev):
    way = 2 - 4 * (lev & 1)
    behind, ahead, far = (lev - way) & 7, (lev + way) & 7, lev ^ 4
    return [lev, behind, ahead, lev ^ 1, ahead ^ 1, behind ^ 1, far, far ^ 1]


def add_up(raw, w_ref, slabs, tabs):
    for slab, tab in zip(slabs, tabs):
        term = mul(w_ref[slab], tab[...], NN)
        raw = term if raw is None else raw + term
    return raw


def near_kernel(lev_ref, w_ref, *refs):
    tabs, raw_ref, turned, same_ref, held, sems = refs[:NEARS], refs[NEARS], refs[NEARS + 1:-3], *refs[-3:]
    places = [same_ref] + [held.at[n] for n in range(NEARS - 1)]
    copies = [pltpu.make_async_copy(tabs[n], places[n], sems.at[n]) for n in range(NEARS)]
    for copy in copies:
        copy.start()
    slabs = slab_order(lev_ref[0])
    raw = None
    for n in range(NEARS):
        copies[n].wait()
        raw = add_up(raw, w_ref, slabs[n:n + 1], places[n:n + 1])
        turned[n][...] = places[n][...].T
    raw_ref[...] = raw


def far_kernel(lev_ref, w_ref, raw_ref, *refs):
    tabs, total_ref, turned = refs[:FARS], refs[FARS], refs[FARS + 1:]
    total_ref[...] = add_up(raw_ref[...], w_ref, slab_order(lev_ref[0])[NEARS:], tabs)
    for tab, turn in zip(tabs, turned):
        turn[...] = tab[...].T


def pass_kernel(token_ref, tab_ref, same_ref):
    pass


def solve_kernel(low_ref, lev_ref, level_ref, w_ref, scale_ref, raw_ref, *refs):
    *tabs, o_ref, out_ref = refs
    low = low_ref[0]
    slabs = slab_order(lev_ref[0])
    wide = add_up(raw_ref[...], w_ref, slabs[7:], tabs[7:])
    kidx = iota((1, KP), 1)
    first = kidx <= CUT - low
    degree = jnp.where(first, low + kidx, kidx - 1).astype(jnp.float32)
    eig = degree * (degree + 1.0) / (CUT * (CUT + 1.0))
    gval = level_ref[0, :, 0:1]
    bval = level_ref[1, :, 0:1]
    spectra = jnp.where(first, wide[:16], wide[16:])
    drive, mass = spectra[:8], spectra[8:]
    solved = (drive - bval * eig * mass) / (1.0 + gval * eig)
    spec = jnp.concatenate([solved, mass + bval * solved], axis=0)
    expanded = jnp.concatenate([jnp.where(first, spec, 0.0), jnp.where(first, 0.0, spec)], axis=0).astype(jnp.bfloat16)
    spread = spread_rows()
    group = own_group()
    for n, slab in enumerate(slabs):
        rows = mul(expanded, tabs[n][...], NN if n < NEARS + FARS else NT)
        rows = jnp.where(members(scale_ref[slab]) > 0.0, rows, 0.0)
        rows = jnp.where(group, jnp.concatenate([rows] * 4, axis=0), 0.0).astype(jnp.bfloat16)
        block = mul(spread, rows, NT)
        place = pl.ds(pl.multiple_of(slab * SLABS, SLABS), SLABS)
        for j in range(STEPS):
            out_ref[j // 5, place, (j % 5) * 128:(j % 5 + 1) * 128] = block[j * SLABS:(j + 1) * SLABS]
    o_ref[...] = jnp.swapaxes(out_ref[...], 0, 1).astype(jnp.bfloat16)


def params(mib):
    return pltpu.CompilerParams(vmem_limit_bytes=mib * 1024 * 1024)


def cost(rows, depth, columns):
    return pl.CostEstimate(flops=2 * max(rows, 256) * depth * columns, transcendentals=0,
                           bytes_accessed=2 * depth * columns)


def chunks():
    return jax.ShapeDtypeStruct((PAIRS, 2, HALF), jnp.bfloat16)


def pack(x, tab):
    return pl.pallas_call(
        pack_kernel, out_shape=(chunks(), like(tab)), in_specs=[ANY, ANY], out_specs=(VMEM, ANY),
        scratch_shapes=[pltpu.VMEM(x.shape, x.dtype), pltpu.VMEM(tab.shape, tab.dtype), pltpu.SemaphoreType.DMA((3,))],
        compiler_params=params(60), cost_estimate=cost(PAIRS * 4, SLAB, 2 * KP), name="pack")(x, tab)


def unpack(b):
    return pl.pallas_call(unpack_kernel, out_shape=jax.ShapeDtypeStruct((F, V, R, 4 * PAIRS), jnp.bfloat16),
                          in_specs=[VMEM], out_specs=VMEM, compiler_params=params(12), cost_estimate=cost(SLAB, PAIRS * 4, 2 * KP),
                          name="unpack")(b)


def coef(low, lev, gamma, beta, points):
    return pl.pallas_call(
        coef_kernel, out_shape=(jax.ShapeDtypeStruct((SLABS, 2, SLAB), jnp.float32),
                                jax.ShapeDtypeStruct((2, SLABS, 128), jnp.float32)),
        in_specs=[SMEM] * 4 + [VMEM], out_specs=(VMEM,) * 2, compiler_params=params(8),
        name="coef")(low, lev, gamma, beta, points)


def like(tab):
    return jax.ShapeDtypeStruct(tab.shape, tab.dtype)


def weigh(y, scale):
    return pl.pallas_call(
        weigh_kernel, out_shape=jax.ShapeDtypeStruct((SLABS, COLS, SLAB), jnp.bfloat16),
        in_specs=[VMEM, VMEM], out_specs=VMEM, compiler_params=params(8),
        cost_estimate=cost(SLABS * 128, SLAB, 128), name="weigh")(y, scale)


def pass_on(token, tab):
    return pl.pallas_call(pass_kernel, out_shape=like(tab), in_specs=[ANY, ANY], out_specs=ANY,
                          input_output_aliases={1: 0}, compiler_params=params(1), name="pass_on")(token, tab)


RAW = jax.ShapeDtypeStruct((COLS, KP), jnp.float32)


TURNED = jax.ShapeDtypeStruct((KP, SLAB), jnp.bfloat16)


def near(lev, w, tabs):
    return pl.pallas_call(
        near_kernel, out_shape=(RAW,) + (TURNED,) * NEARS + (like(tabs[0]),),
        in_specs=[SMEM, VMEM] + [ANY] * NEARS, out_specs=(VMEM,) * (2 + NEARS),
        scratch_shapes=[pltpu.VMEM((NEARS - 1, SLAB, KP), jnp.bfloat16), pltpu.SemaphoreType.DMA((NEARS,))],
        compiler_params=params(12), cost_estimate=pl.CostEstimate(flops=NEAR, bytes_accessed=0, transcendentals=0),
        name="near")(lev, w, *tabs)


def far(lev, w, raw, tabs):
    return pl.pallas_call(
        far_kernel, out_shape=(RAW,) + (TURNED,) * FARS, in_specs=[SMEM] + [VMEM] * (2 + FARS),
        out_specs=(VMEM,) * (1 + FARS),
        compiler_params=params(8), cost_estimate=cost(COLS, 4 * SLAB, KP), name="far")(lev, w, raw, *tabs)


def solve(low, lev, level, w, scale, raw, tabs):
    return pl.pallas_call(
        solve_kernel, out_shape=chunks(), in_specs=[SMEM] * 2 + [VMEM] * (4 + len(tabs)), out_specs=VMEM,
        scratch_shapes=[pltpu.VMEM((2, PAIRS, HALF), jnp.float32)],
        compiler_params=params(12), cost_estimate=cost(COLS, 9 * SLAB, KP),
        name="solve")(low, lev, level, w, scale, raw, *tabs)


def along_x(array, step):
    return lax.ppermute(array, "lev", [(d, (d + 2 * step * (1 - 2 * (d % 2))) % SLABS) for d in range(SLABS)])


def other_core(array):
    return lax.ppermute(array, "lev", [(d, d ^ 1) for d in range(SLABS)])


def local(fourier_in, table, points, pair_low, gamma, beta):
    lev = lax.axis_index("lev").astype(jnp.int32).reshape(1)
    own = jnp.swapaxes(table, 1, 2)[0]
    first = along_x(own, 1)
    sent, own = pack(fourier_in, own)
    second = along_x(own, -1)
    moved = lax.all_to_all(sent, "wave", split_axis=0, concat_axis=0, tiled=True)
    first = pass_on(sent, first)
    third = along_x(first, 1)
    second = pass_on(sent, second)
    cores = [other_core(first), other_core(second)]
    scale, level = coef(pair_low, lev, gamma, beta, points.reshape(1, NLAT))
    weighted = weigh(moved, scale)
    raw, *tabs, own = near(lev, weighted, [own, first, second])
    third = pass_on(raw, third)
    last = other_core(third)
    raw, *more = far(lev, weighted, raw, [other_core(own)] + cores + [third])
    tabs += more + [last]
    result = solve(pair_low, lev, level, weighted, scale, raw, tabs)
    back = lax.all_to_all(result, "wave", split_axis=0, concat_axis=0, tiled=True)
    return unpack(back)


def solution(mesh):
    placed = (P(None, "lev", "wave", None), P("wave", None, "lev"), P(), P("wave"), P(), P())
    return jax.shard_map(
        local, mesh=mesh, in_specs=placed, out_specs=P(None, "lev", "wave", None), check_vma=False
    )
```

```python
import jax
import jax.numpy as jnp
from jax import lax
from jax.experimental import pallas as pl
from jax.experimental.pallas import tpu as pltpu
from jax.sharding import PartitionSpec as P

F = 2
V = 4
R = 40
PAIRS = 64
SLABS = 8
SLAB = 320
KP = 1281
CUT = KP - 2
NLAT = 2560
STEPS = R // 4
COLS = 32
HALF = 640
NEAR = 73 * 10**8
NEARS = 3
FARS = 4

NT = (((1,), (1,)), ((), ()))
NN = (((1,), (0,)), ((), ()))
TN = (((0,), (0,)), ((), ()))
VMEM = pl.BlockSpec(memory_space=pltpu.VMEM)
ANY = pl.BlockSpec(memory_space=pl.ANY)
SMEM = pl.BlockSpec(memory_space=pltpu.SMEM)


def iota(shape, dim):
    return lax.broadcasted_iota(jnp.int32, shape, dim)


def ones_where(cond):
    return jnp.where(cond, 1.0, 0.0).astype(jnp.bfloat16)


def mul(a, b, dims):
    return lax.dot_general(a, b, dims, preferred_element_type=jnp.float32)


def by_member():
    row = iota((4 * PAIRS, 4 * PAIRS), 0)
    return ones_where(iota((4 * PAIRS, 4 * PAIRS), 1) == 4 * (row & (PAIRS - 1)) + (row >> 6))


def by_place():
    lane = iota((1, STEPS * 128), 1)
    source = ((lane >> 3) & 1) * V + ((lane >> 1) & 3)
    source = source * R + 4 * (lane >> 7) + ((lane >> 5) & 3)
    return ones_where(iota((F * V * R, STEPS * 128), 0) == source)


def lane_part(shape):
    lane = iota(shape, 1)
    return ((lane >> 4) & 1) * 2 + (lane & 1)


def pack_kernel(x_ref, tab_ref, o_ref, copy_ref, held_x, held_tab, sems):
    get_x = pltpu.make_async_copy(x_ref, held_x, sems.at[0])
    get_tab = pltpu.make_async_copy(tab_ref, held_tab, sems.at[1])
    put_tab = pltpu.make_async_copy(held_tab, copy_ref, sems.at[2])
    get_x.start()
    get_tab.start()
    get_x.wait()
    x = held_x[...].astype(jnp.float32).reshape(F * V * R, 4 * PAIRS).astype(jnp.bfloat16)
    turned = mul(by_member(), x, NT).astype(jnp.bfloat16)
    get_tab.wait()
    put_tab.start()
    placed = mul(turned, by_place(), NN)
    part = lane_part((PAIRS, STEPS * 128))
    out = placed[:PAIRS]
    for q in range(1, 4):
        out = jnp.where(part == q, placed[q * PAIRS:(q + 1) * PAIRS], out)
    halves = jnp.stack([out[:, :HALF], out[:, HALF:]], axis=0)
    o_ref[...] = jnp.swapaxes(halves, 0, 1).astype(jnp.bfloat16)
    put_tab.wait()


def unpack_kernel(b_ref, o_ref):
    b = jnp.swapaxes(b_ref[...].astype(jnp.float32), 0, 1)
    b = jnp.concatenate([b[0], b[1]], axis=1)
    part = lane_part((PAIRS, STEPS * 128))
    parts = [jnp.where(part == q, b, 0.0).astype(jnp.bfloat16) for q in range(4)]
    turned = mul(by_place(), jnp.concatenate(parts, axis=0), NT).astype(jnp.bfloat16)
    x = mul(turned, by_member(), NN)
    o_ref[...] = x.reshape(F, V, R, 4 * PAIRS).astype(jnp.bfloat16)


def spread_rows():
    row = iota((STEPS * SLABS, SLAB), 0)
    gap = iota((STEPS * SLABS, SLAB), 1) - (row & 7) * R - 4 * (row >> 3)
    return ones_where((gap >= 0) & (gap < 4))


def place_rows():
    lane = iota((1, 512), 1)
    row = (lane & 7) * R + 4 * ((lane >> 3) & 15) + (lane >> 7)
    return ones_where((iota((SLAB, 512), 0) == row) & (((lane >> 3) & 15) < STEPS))


def own_group():
    return (iota((4 * COLS, SLAB), 0) >> 5) == (iota((4 * COLS, SLAB), 1) & 3)


def coef_kernel(low_ref, lev_ref, gamma_ref, beta_ref, points_ref, token_ref, scale_ref, level_ref):
    low = low_ref[0]
    points = jnp.concatenate([points_ref[:, s * SLAB:(s + 1) * SLAB] for s in range(SLABS)], axis=0)
    pts = points.astype(jnp.float32)
    weights = NLAT * pts / jnp.sum(pts)
    limit = jnp.minimum(CUT, (points >> 1) - 1)
    rows = jnp.stack([jnp.where(low <= limit, weights, 0.0), jnp.where(CUT - low <= limit, weights, 0.0)], axis=0)
    for s in range(SLABS):
        scale_ref[s] = rows[:, s, :]
    level = iota((SLABS, 128), 0) >> 1
    gval = jnp.zeros((SLABS, 128), jnp.float32)
    bval = jnp.zeros((SLABS, 128), jnp.float32)
    for v in range(V):
        gval = jnp.where(level == v, gamma_ref[lev_ref[0] * V + v], gval)
        bval = jnp.where(level == v, beta_ref[lev_ref[0] * V + v], bval)
    level_ref[0] = gval
    level_ref[1] = bval


def members(pair):
    return jnp.concatenate([jnp.broadcast_to(pair[m:m + 1], (COLS // 2, SLAB)) for m in range(2)], axis=0)


def weigh_kernel(y_ref, scale_ref, o_ref):
    spread = spread_rows()
    group = own_group()
    y = jnp.swapaxes(y_ref[...].astype(jnp.float32), 0, 1)
    for s in range(SLABS):
        rows = y[:, s * SLABS:(s + 1) * SLABS]
        block = jnp.concatenate([rows[j // 5, :, (j % 5) * 128:(j % 5 + 1) * 128] for j in range(STEPS)], axis=0)
        turned = jnp.where(group, mul(block.astype(jnp.bfloat16), spread, TN), 0.0)
        turned = turned[:32] + turned[32:64] + turned[64:96] + turned[96:]
        o_ref[s] = (turned * members(scale_ref[s])).astype(jnp.bfloat16)


def slab_order(lev):
    way = 2 - 4 * (lev & 1)
    behind, ahead, far = (lev - way) & 7, (lev + way) & 7, lev ^ 4
    return [lev, behind, ahead, lev ^ 1, ahead ^ 1, behind ^ 1, far, far ^ 1]


def add_up(raw, w_ref, slabs, tabs):
    for slab, tab in zip(slabs, tabs):
        term = mul(w_ref[slab], tab[...], NN)
        raw = term if raw is None else raw + term
    return raw


def near_kernel(lev_ref, w_ref, *refs):
    tabs, raw_ref, turned, same_ref, held, sems = refs[:NEARS], refs[NEARS], refs[NEARS + 1:-3], *refs[-3:]
    places = [same_ref] + [held.at[n] for n in range(NEARS - 1)]
    copies = [pltpu.make_async_copy(tabs[n], places[n], sems.at[n]) for n in range(NEARS)]
    for copy in copies:
        copy.start()
    slabs = slab_order(lev_ref[0])
    raw = None
    for n in range(NEARS):
        copies[n].wait()
        raw = add_up(raw, w_ref, slabs[n:n + 1], places[n:n + 1])
        turned[n][...] = places[n][...].T
    raw_ref[...] = raw


def far_kernel(lev_ref, w_ref, raw_ref, *refs):
    tabs, total_ref, turned = refs[:FARS], refs[FARS], refs[FARS + 1:]
    total_ref[...] = add_up(raw_ref[...], w_ref, slab_order(lev_ref[0])[NEARS:], tabs)
    for tab, turn in zip(tabs, turned):
        turn[...] = tab[...].T


def pass_kernel(token_ref, tab_ref, same_ref):
    pass


def solve_kernel(low_ref, lev_ref, level_ref, w_ref, scale_ref, raw_ref, *refs):
    *tabs, o_ref, out_ref = refs
    low = low_ref[0]
    slabs = slab_order(lev_ref[0])
    wide = add_up(raw_ref[...], w_ref, slabs[7:], tabs[7:])
    kidx = iota((1, KP), 1)
    first = kidx <= CUT - low
    degree = jnp.where(first, low + kidx, kidx - 1).astype(jnp.float32)
    eig = degree * (degree + 1.0) / (CUT * (CUT + 1.0))
    gval = level_ref[0, :, 0:1]
    bval = level_ref[1, :, 0:1]
    spectra = jnp.where(first, wide[:16], wide[16:])
    drive, mass = spectra[:8], spectra[8:]
    solved = (drive - bval * eig * mass) / (1.0 + gval * eig)
    spec = jnp.concatenate([solved, mass + bval * solved], axis=0)
    expanded = jnp.concatenate([jnp.where(first, spec, 0.0), jnp.where(first, 0.0, spec)], axis=0).astype(jnp.bfloat16)
    rows = []
    for n, slab in enumerate(slabs):
        part = mul(expanded, tabs[n][...], NN if n < NEARS + FARS else NT)
        rows.append(jnp.where(members(scale_ref[slab]) > 0.0, part, 0.0).astype(jnp.bfloat16))
    placed = mul(jnp.concatenate(rows, axis=0), place_rows(), NN)
    for n, slab in enumerate(slabs):
        part = placed[n * COLS:(n + 1) * COLS]
        block = jnp.concatenate([part[:, g * 128:(g + 1) * 128] for g in range(4)], axis=0).T
        place = pl.ds(pl.multiple_of(slab * SLABS, SLABS), SLABS)
        for j in range(STEPS):
            out_ref[j // 5, place, (j % 5) * 128:(j % 5 + 1) * 128] = block[j * SLABS:(j + 1) * SLABS]
    o_ref[...] = jnp.swapaxes(out_ref[...], 0, 1).astype(jnp.bfloat16)


def params(mib):
    return pltpu.CompilerParams(vmem_limit_bytes=mib * 1024 * 1024)


def cost(rows, depth, columns):
    return pl.CostEstimate(flops=2 * max(rows, 256) * depth * columns, transcendentals=0,
                           bytes_accessed=2 * depth * columns)


def chunks():
    return jax.ShapeDtypeStruct((PAIRS, 2, HALF), jnp.bfloat16)


def pack(x, tab):
    return pl.pallas_call(
        pack_kernel, out_shape=(chunks(), like(tab)), in_specs=[ANY, ANY], out_specs=(VMEM, ANY),
        scratch_shapes=[pltpu.VMEM(x.shape, x.dtype), pltpu.VMEM(tab.shape, tab.dtype), pltpu.SemaphoreType.DMA((3,))],
        compiler_params=params(60), cost_estimate=cost(PAIRS * 4, SLAB, 2 * KP), name="pack")(x, tab)


def unpack(b):
    return pl.pallas_call(unpack_kernel, out_shape=jax.ShapeDtypeStruct((F, V, R, 4 * PAIRS), jnp.bfloat16),
                          in_specs=[VMEM], out_specs=VMEM, compiler_params=params(12), cost_estimate=cost(SLAB, PAIRS * 4, 2 * KP),
                          name="unpack")(b)


def coef(low, lev, gamma, beta, points, token):
    return pl.pallas_call(
        coef_kernel, out_shape=(jax.ShapeDtypeStruct((SLABS, 2, SLAB), jnp.float32),
                                jax.ShapeDtypeStruct((2, SLABS, 128), jnp.float32)),
        in_specs=[SMEM] * 4 + [VMEM, ANY], out_specs=(VMEM,) * 2, compiler_params=params(8),
        name="coef")(low, lev, gamma, beta, points, token)


def like(tab):
    return jax.ShapeDtypeStruct(tab.shape, tab.dtype)


def weigh(y, scale):
    return pl.pallas_call(
        weigh_kernel, out_shape=jax.ShapeDtypeStruct((SLABS, COLS, SLAB), jnp.bfloat16),
        in_specs=[VMEM, VMEM], out_specs=VMEM, compiler_params=params(8),
        cost_estimate=cost(SLABS * 128, SLAB, 128), name="weigh")(y, scale)


def pass_on(token, tab):
    return pl.pallas_call(pass_kernel, out_shape=like(tab), in_specs=[ANY, ANY], out_specs=ANY,
                          input_output_aliases={1: 0}, compiler_params=params(1), name="pass_on")(token, tab)


RAW = jax.ShapeDtypeStruct((COLS, KP), jnp.float32)


TURNED = jax.ShapeDtypeStruct((KP, SLAB), jnp.bfloat16)


def near(lev, w, tabs):
    return pl.pallas_call(
        near_kernel, out_shape=(RAW,) + (TURNED,) * NEARS + (like(tabs[0]),),
        in_specs=[SMEM, VMEM] + [ANY] * NEARS, out_specs=(VMEM,) * (2 + NEARS),
        scratch_shapes=[pltpu.VMEM((NEARS - 1, SLAB, KP), jnp.bfloat16), pltpu.SemaphoreType.DMA((NEARS,))],
        compiler_params=params(12), cost_estimate=pl.CostEstimate(flops=NEAR, bytes_accessed=0, transcendentals=0),
        name="near")(lev, w, *tabs)


def far(lev, w, raw, tabs):
    return pl.pallas_call(
        far_kernel, out_shape=(RAW,) + (TURNED,) * FARS, in_specs=[SMEM] + [VMEM] * (2 + FARS),
        out_specs=(VMEM,) * (1 + FARS),
        compiler_params=params(8), cost_estimate=cost(COLS, 4 * SLAB, KP), name="far")(lev, w, raw, *tabs)


def solve(low, lev, level, w, scale, raw, tabs):
    return pl.pallas_call(
        solve_kernel, out_shape=chunks(), in_specs=[SMEM] * 2 + [VMEM] * (4 + len(tabs)), out_specs=VMEM,
        scratch_shapes=[pltpu.VMEM((2, PAIRS, HALF), jnp.float32)],
        compiler_params=params(12), cost_estimate=cost(COLS, 9 * SLAB, KP),
        name="solve")(low, lev, level, w, scale, raw, *tabs)


def along_x(array, step):
    return lax.ppermute(array, "lev", [(d, (d + 2 * step * (1 - 2 * (d % 2))) % SLABS) for d in range(SLABS)])


def other_core(array):
    return lax.ppermute(array, "lev", [(d, d ^ 1) for d in range(SLABS)])


def local(fourier_in, table, points, pair_low, gamma, beta):
    lev = lax.axis_index("lev").astype(jnp.int32).reshape(1)
    own = jnp.swapaxes(table, 1, 2)[0]
    first = along_x(own, 1)
    sent, copied = pack(fourier_in, own)
    second = along_x(copied, -1)
    moved = lax.all_to_all(sent, "wave", split_axis=0, concat_axis=0, tiled=True)
    scale, level = coef(pair_low, lev, gamma, beta, points.reshape(1, NLAT), sent)
    first = pass_on(level, first)
    third = along_x(first, 1)
    second = pass_on(sent, second)
    cores = [other_core(first), other_core(second)]
    weighted = weigh(moved, scale)
    raw, *tabs, own = near(lev, weighted, [own, first, second])
    third = pass_on(raw, third)
    last = other_core(third)
    raw, *more = far(lev, weighted, raw, [other_core(own)] + cores + [third])
    tabs += more + [last]
    result = solve(pair_low, lev, level, weighted, scale, raw, tabs)
    back = lax.all_to_all(result, "wave", split_axis=0, concat_axis=0, tiled=True)
    return unpack(back)


def solution(mesh):
    placed = (P(None, "lev", "wave", None), P("wave", None, "lev"), P(), P("wave"), P(), P())
    return jax.shard_map(
        local, mesh=mesh, in_specs=placed, out_specs=P(None, "lev", "wave", None), check_vma=False
    )
```

```python
import jax
import jax.numpy as jnp
from jax import lax
from jax.experimental import pallas as pl
from jax.experimental.pallas import tpu as pltpu
from jax.sharding import PartitionSpec as P

F = 2
V = 4
R = 40
PAIRS = 64
SLABS = 8
SLAB = 320
KP = 1281
CUT = KP - 2
NLAT = 2560
STEPS = R // 4
COLS = 32
HALF = 640
NEAR = 73 * 10**8
NEARS = 3
FARS = 4

NT = (((1,), (1,)), ((), ()))
NN = (((1,), (0,)), ((), ()))
TN = (((0,), (0,)), ((), ()))
VMEM = pl.BlockSpec(memory_space=pltpu.VMEM)
ANY = pl.BlockSpec(memory_space=pl.ANY)
SMEM = pl.BlockSpec(memory_space=pltpu.SMEM)


def iota(shape, dim):
    return lax.broadcasted_iota(jnp.int32, shape, dim)


def ones_where(cond):
    return jnp.where(cond, 1.0, 0.0).astype(jnp.bfloat16)


def mul(a, b, dims):
    return lax.dot_general(a, b, dims, preferred_element_type=jnp.float32)


def by_member():
    row = iota((4 * PAIRS, 4 * PAIRS), 0)
    return ones_where(iota((4 * PAIRS, 4 * PAIRS), 1) == 4 * (row & (PAIRS - 1)) + (row >> 6))


def by_place():
    lane = iota((1, STEPS * 128), 1)
    source = ((lane >> 3) & 1) * V + ((lane >> 1) & 3)
    source = source * R + 4 * (lane >> 7) + ((lane >> 5) & 3)
    return ones_where(iota((F * V * R, STEPS * 128), 0) == source)


def by_place_turned():
    row = iota((STEPS * 128, 1), 0)
    source = ((row >> 3) & 1) * V + ((row >> 1) & 3)
    source = source * R + 4 * (row >> 7) + ((row >> 5) & 3)
    return ones_where(iota((STEPS * 128, F * V * R), 1) == source)


def lane_part(shape):
    lane = iota(shape, 1)
    return ((lane >> 4) & 1) * 2 + (lane & 1)


def pack_kernel(x_ref, tab_ref, o_ref, copy_ref, held_x, held_tab, sems):
    get_x = pltpu.make_async_copy(x_ref, held_x, sems.at[0])
    get_tab = pltpu.make_async_copy(tab_ref, held_tab, sems.at[1])
    put_tab = pltpu.make_async_copy(held_tab, copy_ref, sems.at[2])
    get_x.start()
    get_tab.start()
    get_x.wait()
    x = held_x[...].astype(jnp.float32).reshape(F * V * R, 4 * PAIRS).astype(jnp.bfloat16)
    turned = mul(by_member(), x, NT).astype(jnp.bfloat16)
    get_tab.wait()
    put_tab.start()
    placed = mul(turned, by_place(), NN)
    part = lane_part((PAIRS, STEPS * 128))
    out = placed[:PAIRS]
    for q in range(1, 4):
        out = jnp.where(part == q, placed[q * PAIRS:(q + 1) * PAIRS], out)
    halves = jnp.stack([out[:, :HALF], out[:, HALF:]], axis=0)
    o_ref[...] = jnp.swapaxes(halves, 0, 1).astype(jnp.bfloat16)
    put_tab.wait()


def unpack_kernel(b_ref, o_ref):
    b = jnp.swapaxes(b_ref[...].astype(jnp.float32), 0, 1)
    b = jnp.concatenate([b[0], b[1]], axis=1).astype(jnp.bfloat16)
    part = lane_part((1, STEPS * 128))
    parts = [b * ones_where(part == q) for q in range(4)]
    turned = mul(jnp.concatenate(parts, axis=0), by_place_turned(), NN).astype(jnp.bfloat16)
    x = mul(turned, by_member(), TN)
    o_ref[...] = x.reshape(F, V, R, 4 * PAIRS).astype(jnp.bfloat16)


def spread_rows():
    row = iota((STEPS * SLABS, SLAB), 0)
    gap = iota((STEPS * SLABS, SLAB), 1) - (row & 7) * R - 4 * (row >> 3)
    return ones_where((gap >= 0) & (gap < 4))


def place_rows():
    lane = iota((1, 512), 1)
    row = (lane & 7) * R + 4 * ((lane >> 3) & 15) + (lane >> 7)
    return ones_where((iota((SLAB, 512), 0) == row) & (((lane >> 3) & 15) < STEPS))


def own_group():
    return (iota((4 * COLS, SLAB), 0) >> 5) == (iota((4 * COLS, SLAB), 1) & 3)


def coef_kernel(low_ref, lev_ref, gamma_ref, beta_ref, points_ref, token_ref, scale_ref, level_ref):
    low = low_ref[0]
    points = jnp.concatenate([points_ref[:, s * SLAB:(s + 1) * SLAB] for s in range(SLABS)], axis=0)
    pts = points.astype(jnp.float32)
    weights = NLAT * pts / jnp.sum(pts)
    limit = jnp.minimum(CUT, (points >> 1) - 1)
    rows = jnp.stack([jnp.where(low <= limit, weights, 0.0), jnp.where(CUT - low <= limit, weights, 0.0)], axis=0)
    for s in range(SLABS):
        scale_ref[s] = rows[:, s, :]
    level = iota((SLABS, 128), 0) >> 1
    gval = jnp.zeros((SLABS, 128), jnp.float32)
    bval = jnp.zeros((SLABS, 128), jnp.float32)
    for v in range(V):
        gval = jnp.where(level == v, gamma_ref[lev_ref[0] * V + v], gval)
        bval = jnp.where(level == v, beta_ref[lev_ref[0] * V + v], bval)
    level_ref[0] = gval
    level_ref[1] = bval


def members(pair):
    return jnp.concatenate([jnp.broadcast_to(pair[m:m + 1], (COLS // 2, SLAB)) for m in range(2)], axis=0)


def weigh_kernel(y_ref, scale_ref, o_ref):
    spread = spread_rows()
    group = own_group()
    y = jnp.swapaxes(y_ref[...].astype(jnp.float32), 0, 1)
    for s in range(SLABS):
        rows = y[:, s * SLABS:(s + 1) * SLABS]
        block = jnp.concatenate([rows[j // 5, :, (j % 5) * 128:(j % 5 + 1) * 128] for j in range(STEPS)], axis=0)
        turned = jnp.where(group, mul(block.astype(jnp.bfloat16), spread, TN), 0.0)
        turned = turned[:32] + turned[32:64] + turned[64:96] + turned[96:]
        o_ref[s] = (turned * members(scale_ref[s])).astype(jnp.bfloat16)


def slab_order(lev):
    way = 2 - 4 * (lev & 1)
    behind, ahead, far = (lev - way) & 7, (lev + way) & 7, lev ^ 4
    return [lev, behind, ahead, lev ^ 1, ahead ^ 1, behind ^ 1, far, far ^ 1]


def add_up(raw, w_ref, slabs, tabs):
    for slab, tab in zip(slabs, tabs):
        term = mul(w_ref[slab], tab[...], NN)
        raw = term if raw is None else raw + term
    return raw


def near_kernel(lev_ref, w_ref, *refs):
    tabs, raw_ref, turned, same_ref, held, sems = refs[:NEARS], refs[NEARS], refs[NEARS + 1:-3], *refs[-3:]
    places = [same_ref] + [held.at[n] for n in range(NEARS - 1)]
    copies = [pltpu.make_async_copy(tabs[n], places[n], sems.at[n]) for n in range(NEARS)]
    for copy in copies:
        copy.start()
    slabs = slab_order(lev_ref[0])
    raw = None
    for n in range(NEARS):
        copies[n].wait()
        raw = add_up(raw, w_ref, slabs[n:n + 1], places[n:n + 1])
        turned[n][...] = places[n][...].T
    raw_ref[...] = raw


def far_kernel(lev_ref, w_ref, raw_ref, *refs):
    tabs, total_ref, turned = refs[:FARS], refs[FARS], refs[FARS + 1:]
    total_ref[...] = add_up(raw_ref[...], w_ref, slab_order(lev_ref[0])[NEARS:], tabs)
    for tab, turn in zip(tabs, turned):
        turn[...] = tab[...].T


def pass_kernel(token_ref, tab_ref, same_ref):
    pass


def solve_kernel(low_ref, lev_ref, level_ref, w_ref, scale_ref, raw_ref, *refs):
    *tabs, o_ref, out_ref = refs
    low = low_ref[0]
    slabs = slab_order(lev_ref[0])
    wide = add_up(raw_ref[...], w_ref, slabs[7:], tabs[7:])
    kidx = iota((1, KP), 1)
    first = kidx <= CUT - low
    degree = jnp.where(first, low + kidx, kidx - 1).astype(jnp.float32)
    eig = degree * (degree + 1.0) / (CUT * (CUT + 1.0))
    gval = level_ref[0, :, 0:1]
    bval = level_ref[1, :, 0:1]
    spectra = jnp.where(first, wide[:16], wide[16:])
    drive, mass = spectra[:8], spectra[8:]
    solved = (drive - bval * eig * mass) / (1.0 + gval * eig)
    spec = jnp.concatenate([solved, mass + bval * solved], axis=0)
    expanded = jnp.concatenate([jnp.where(first, spec, 0.0), jnp.where(first, 0.0, spec)], axis=0).astype(jnp.bfloat16)
    rows = []
    for n, slab in enumerate(slabs):
        part = mul(expanded, tabs[n][...], NN if n < NEARS + FARS else NT)
        rows.append(jnp.where(members(scale_ref[slab]) > 0.0, part, 0.0).astype(jnp.bfloat16))
    placed = mul(jnp.concatenate(rows, axis=0), place_rows(), NN)
    for n, slab in enumerate(slabs):
        part = placed[n * COLS:(n + 1) * COLS]
        block = jnp.concatenate([part[:, g * 128:(g + 1) * 128] for g in range(4)], axis=0).T
        place = pl.ds(pl.multiple_of(slab * SLABS, SLABS), SLABS)
        for j in range(STEPS):
            out_ref[j // 5, place, (j % 5) * 128:(j % 5 + 1) * 128] = block[j * SLABS:(j + 1) * SLABS]
    o_ref[...] = jnp.swapaxes(out_ref[...], 0, 1).astype(jnp.bfloat16)


def params(mib):
    return pltpu.CompilerParams(vmem_limit_bytes=mib * 1024 * 1024)


def cost(rows, depth, columns):
    return pl.CostEstimate(flops=2 * max(rows, 256) * depth * columns, transcendentals=0,
                           bytes_accessed=2 * depth * columns)


def chunks():
    return jax.ShapeDtypeStruct((PAIRS, 2, HALF), jnp.bfloat16)


def pack(x, tab):
    return pl.pallas_call(
        pack_kernel, out_shape=(chunks(), like(tab)), in_specs=[ANY, ANY], out_specs=(VMEM, ANY),
        scratch_shapes=[pltpu.VMEM(x.shape, x.dtype), pltpu.VMEM(tab.shape, tab.dtype), pltpu.SemaphoreType.DMA((3,))],
        compiler_params=params(60), cost_estimate=cost(PAIRS * 4, SLAB, 2 * KP), name="pack")(x, tab)


def unpack(b):
    return pl.pallas_call(unpack_kernel, out_shape=jax.ShapeDtypeStruct((F, V, R, 4 * PAIRS), jnp.bfloat16),
                          in_specs=[VMEM], out_specs=VMEM, compiler_params=params(12), cost_estimate=cost(SLAB, PAIRS * 4, 2 * KP),
                          name="unpack")(b)


def coef(low, lev, gamma, beta, points, token):
    return pl.pallas_call(
        coef_kernel, out_shape=(jax.ShapeDtypeStruct((SLABS, 2, SLAB), jnp.float32),
                                jax.ShapeDtypeStruct((2, SLABS, 128), jnp.float32)),
        in_specs=[SMEM] * 4 + [VMEM, ANY], out_specs=(VMEM,) * 2, compiler_params=params(8),
        name="coef")(low, lev, gamma, beta, points, token)


def like(tab):
    return jax.ShapeDtypeStruct(tab.shape, tab.dtype)


def weigh(y, scale):
    return pl.pallas_call(
        weigh_kernel, out_shape=jax.ShapeDtypeStruct((SLABS, COLS, SLAB), jnp.bfloat16),
        in_specs=[VMEM, VMEM], out_specs=VMEM, compiler_params=params(8),
        cost_estimate=cost(SLABS * 128, SLAB, 128), name="weigh")(y, scale)


def pass_on(token, tab):
    return pl.pallas_call(pass_kernel, out_shape=like(tab), in_specs=[ANY, ANY], out_specs=ANY,
                          input_output_aliases={1: 0}, compiler_params=params(1), name="pass_on")(token, tab)


RAW = jax.ShapeDtypeStruct((COLS, KP), jnp.float32)


TURNED = jax.ShapeDtypeStruct((KP, SLAB), jnp.bfloat16)


def near(lev, w, tabs):
    return pl.pallas_call(
        near_kernel, out_shape=(RAW,) + (TURNED,) * NEARS + (like(tabs[0]),),
        in_specs=[SMEM, VMEM] + [ANY] * NEARS, out_specs=(VMEM,) * (2 + NEARS),
        scratch_shapes=[pltpu.VMEM((NEARS - 1, SLAB, KP), jnp.bfloat16), pltpu.SemaphoreType.DMA((NEARS,))],
        compiler_params=params(12), cost_estimate=pl.CostEstimate(flops=NEAR, bytes_accessed=0, transcendentals=0),
        name="near")(lev, w, *tabs)


def far(lev, w, raw, tabs):
    return pl.pallas_call(
        far_kernel, out_shape=(RAW,) + (TURNED,) * FARS, in_specs=[SMEM] + [VMEM] * (2 + FARS),
        out_specs=(VMEM,) * (1 + FARS),
        compiler_params=params(8), cost_estimate=cost(COLS, 4 * SLAB, KP), name="far")(lev, w, raw, *tabs)


def solve(low, lev, level, w, scale, raw, tabs):
    return pl.pallas_call(
        solve_kernel, out_shape=chunks(), in_specs=[SMEM] * 2 + [VMEM] * (4 + len(tabs)), out_specs=VMEM,
        scratch_shapes=[pltpu.VMEM((2, PAIRS, HALF), jnp.float32)],
        compiler_params=params(12), cost_estimate=cost(COLS, 9 * SLAB, KP),
        name="solve")(low, lev, level, w, scale, raw, *tabs)


def along_x(array, step):
    return lax.ppermute(array, "lev", [(d, (d + 2 * step * (1 - 2 * (d % 2))) % SLABS) for d in range(SLABS)])


def other_core(array):
    return lax.ppermute(array, "lev", [(d, d ^ 1) for d in range(SLABS)])


def local(fourier_in, table, points, pair_low, gamma, beta):
    lev = lax.axis_index("lev").astype(jnp.int32).reshape(1)
    own = jnp.swapaxes(table, 1, 2)[0]
    first = along_x(own, 1)
    sent, copied = pack(fourier_in, own)
    second = along_x(copied, -1)
    moved = lax.all_to_all(sent, "wave", split_axis=0, concat_axis=0, tiled=True)
    scale, level = coef(pair_low, lev, gamma, beta, points.reshape(1, NLAT), sent)
    first = pass_on(level, first)
    third = along_x(first, 1)
    second = pass_on(sent, second)
    cores = [other_core(first), other_core(second)]
    weighted = weigh(moved, scale)
    raw, *tabs, own = near(lev, weighted, [own, first, second])
    third = pass_on(raw, third)
    last = other_core(third)
    raw, *more = far(lev, weighted, raw, [other_core(own)] + cores + [third])
    tabs += more + [last]
    result = solve(pair_low, lev, level, weighted, scale, raw, tabs)
    back = lax.all_to_all(result, "wave", split_axis=0, concat_axis=0, tiled=True)
    return unpack(back)


def solution(mesh):
    placed = (P(None, "lev", "wave", None), P("wave", None, "lev"), P(), P("wave"), P(), P())
    return jax.shard_map(
        local, mesh=mesh, in_specs=placed, out_specs=P(None, "lev", "wave", None), check_vma=False
    )
```

```python
import jax
import jax.numpy as jnp
from jax import lax
from jax.experimental import pallas as pl
from jax.experimental.pallas import tpu as pltpu
from jax.sharding import PartitionSpec as P

F = 2
V = 4
R = 40
PAIRS = 64
SLABS = 8
SLAB = 320
KP = 1281
CUT = KP - 2
NLAT = 2560
STEPS = R // 4
COLS = 32
HALF = 640
NEAR = 75 * 10**8
NEARS = 3
FARS = 4

NT = (((1,), (1,)), ((), ()))
NN = (((1,), (0,)), ((), ()))
TN = (((0,), (0,)), ((), ()))
VMEM = pl.BlockSpec(memory_space=pltpu.VMEM)
ANY = pl.BlockSpec(memory_space=pl.ANY)
SMEM = pl.BlockSpec(memory_space=pltpu.SMEM)


def iota(shape, dim):
    return lax.broadcasted_iota(jnp.int32, shape, dim)


def ones_where(cond):
    return jnp.where(cond, 1.0, 0.0).astype(jnp.bfloat16)


def mul(a, b, dims):
    return lax.dot_general(a, b, dims, preferred_element_type=jnp.float32)


def by_member():
    row = iota((4 * PAIRS, 4 * PAIRS), 0)
    return ones_where(iota((4 * PAIRS, 4 * PAIRS), 1) == 4 * (row & (PAIRS - 1)) + (row >> 6))


def by_place():
    lane = iota((1, STEPS * 128), 1)
    source = ((lane >> 3) & 1) * V + ((lane >> 1) & 3)
    source = source * R + 4 * (lane >> 7) + ((lane >> 5) & 3)
    return ones_where(iota((F * V * R, STEPS * 128), 0) == source)


def lane_part(shape):
    lane = iota(shape, 1)
    return ((lane >> 4) & 1) * 2 + (lane & 1)


def pack_kernel(x_ref, tab_ref, o_ref, copy_ref, held_x, held_tab, sems):
    get_x = pltpu.make_async_copy(x_ref, held_x, sems.at[0])
    get_tab = pltpu.make_async_copy(tab_ref, held_tab, sems.at[1])
    put_tab = pltpu.make_async_copy(held_tab, copy_ref, sems.at[2])
    get_x.start()
    get_tab.start()
    get_x.wait()
    x = held_x[...].astype(jnp.float32).reshape(F * V * R, 4 * PAIRS).astype(jnp.bfloat16)
    turned = mul(by_member(), x, NT).astype(jnp.bfloat16)
    get_tab.wait()
    put_tab.start()
    placed = mul(turned, by_place(), NN)
    part = lane_part((PAIRS, STEPS * 128))
    out = placed[:PAIRS]
    for q in range(1, 4):
        out = jnp.where(part == q, placed[q * PAIRS:(q + 1) * PAIRS], out)
    halves = jnp.stack([out[:, :HALF], out[:, HALF:]], axis=0)
    o_ref[...] = jnp.swapaxes(halves, 0, 1).astype(jnp.bfloat16)
    put_tab.wait()


def unpack_kernel(b_ref, o_ref):
    b = jnp.swapaxes(b_ref[...].astype(jnp.float32), 0, 1)
    b = jnp.concatenate([b[0], b[1]], axis=1)
    part = lane_part((PAIRS, STEPS * 128))
    parts = [jnp.where(part == q, b, 0.0).astype(jnp.bfloat16) for q in range(4)]
    turned = mul(by_place(), jnp.concatenate(parts, axis=0), NT).astype(jnp.bfloat16)
    x = mul(turned, by_member(), NN)
    o_ref[...] = x.reshape(F, V, R, 4 * PAIRS).astype(jnp.bfloat16)


def spread_rows():
    row = iota((STEPS * SLABS, SLAB), 0)
    gap = iota((STEPS * SLABS, SLAB), 1) - (row & 7) * R - 4 * (row >> 3)
    return ones_where((gap >= 0) & (gap < 4))


def place_rows():
    lane = iota((1, 512), 1)
    row = (lane & 7) * R + 4 * ((lane >> 3) & 15) + (lane >> 7)
    return ones_where((iota((SLAB, 512), 0) == row) & (((lane >> 3) & 15) < STEPS))


def own_group():
    return (iota((4 * COLS, SLAB), 0) >> 5) == (iota((4 * COLS, SLAB), 1) & 3)


def coef_kernel(low_ref, lev_ref, gamma_ref, beta_ref, points_ref, token_ref, scale_ref, level_ref):
    low = low_ref[0]
    points = jnp.concatenate([points_ref[:, s * SLAB:(s + 1) * SLAB] for s in range(SLABS)], axis=0)
    pts = points.astype(jnp.float32)
    weights = NLAT * pts / jnp.sum(pts)
    limit = jnp.minimum(CUT, (points >> 1) - 1)
    rows = jnp.stack([jnp.where(low <= limit, weights, 0.0), jnp.where(CUT - low <= limit, weights, 0.0)], axis=0)
    for s in range(SLABS):
        scale_ref[s] = rows[:, s, :]
    level = iota((SLABS, 128), 0) >> 1
    gval = jnp.zeros((SLABS, 128), jnp.float32)
    bval = jnp.zeros((SLABS, 128), jnp.float32)
    for v in range(V):
        gval = jnp.where(level == v, gamma_ref[lev_ref[0] * V + v], gval)
        bval = jnp.where(level == v, beta_ref[lev_ref[0] * V + v], bval)
    level_ref[0] = gval
    level_ref[1] = bval


def members(pair):
    return jnp.concatenate([jnp.broadcast_to(pair[m:m + 1], (COLS // 2, SLAB)) for m in range(2)], axis=0)


def weigh_kernel(y_ref, scale_ref, o_ref):
    spread = spread_rows()
    group = own_group()
    y = jnp.swapaxes(y_ref[...].astype(jnp.float32), 0, 1)
    for s in range(SLABS):
        rows = y[:, s * SLABS:(s + 1) * SLABS]
        block = jnp.concatenate([rows[j // 5, :, (j % 5) * 128:(j % 5 + 1) * 128] for j in range(STEPS)], axis=0)
        turned = jnp.where(group, mul(block.astype(jnp.bfloat16), spread, TN), 0.0)
        turned = turned[:32] + turned[32:64] + turned[64:96] + turned[96:]
        o_ref[s] = (turned * members(scale_ref[s])).astype(jnp.bfloat16)


def slab_order(lev):
    way = 2 - 4 * (lev & 1)
    behind, ahead, far = (lev - way) & 7, (lev + way) & 7, lev ^ 4
    return [lev, behind, ahead, lev ^ 1, ahead ^ 1, behind ^ 1, far, far ^ 1]


def add_up(raw, w_ref, slabs, tabs):
    for slab, tab in zip(slabs, tabs):
        term = mul(w_ref[slab], tab[...], NN)
        raw = term if raw is None else raw + term
    return raw


def near_kernel(lev_ref, w_ref, *refs):
    tabs, raw_ref, turned, held, sems = refs[:NEARS], refs[NEARS], refs[NEARS + 1:-2], *refs[-2:]
    copies = [pltpu.make_async_copy(tabs[n], held.at[n], sems.at[n]) for n in range(NEARS)]
    for copy in copies:
        copy.start()
    slabs = slab_order(lev_ref[0])
    raw = None
    for n in range(NEARS):
        copies[n].wait()
        raw = add_up(raw, w_ref, slabs[n:n + 1], [held.at[n]])
        turned[n][...] = held[n].T
    raw_ref[...] = raw


def far_kernel(lev_ref, w_ref, raw_ref, *refs):
    tabs, total_ref, turned = refs[:FARS], refs[FARS], refs[FARS + 1:]
    total_ref[...] = add_up(raw_ref[...], w_ref, slab_order(lev_ref[0])[NEARS:], tabs)
    for tab, turn in zip(tabs, turned):
        turn[...] = tab[...].T


def pass_kernel(token_ref, tab_ref, same_ref):
    pass


def solve_kernel(low_ref, lev_ref, level_ref, w_ref, scale_ref, raw_ref, *refs):
    *tabs, o_ref, out_ref = refs
    low = low_ref[0]
    slabs = slab_order(lev_ref[0])
    wide = add_up(raw_ref[...], w_ref, slabs[7:], tabs[7:])
    kidx = iota((1, KP), 1)
    first = kidx <= CUT - low
    degree = jnp.where(first, low + kidx, kidx - 1).astype(jnp.float32)
    eig = degree * (degree + 1.0) / (CUT * (CUT + 1.0))
    gval = level_ref[0, :, 0:1]
    bval = level_ref[1, :, 0:1]
    spectra = jnp.where(first, wide[:16], wide[16:])
    drive, mass = spectra[:8], spectra[8:]
    solved = (drive - bval * eig * mass) / (1.0 + gval * eig)
    spec = jnp.concatenate([solved, mass + bval * solved], axis=0)
    expanded = jnp.concatenate([jnp.where(first, spec, 0.0), jnp.where(first, 0.0, spec)], axis=0).astype(jnp.bfloat16)
    rows = []
    for n, slab in enumerate(slabs):
        part = mul(expanded, tabs[n][...], NN if n < NEARS + FARS else NT)
        rows.append(jnp.where(members(scale_ref[slab]) > 0.0, part, 0.0).astype(jnp.bfloat16))
    placed = mul(jnp.concatenate(rows, axis=0), place_rows(), NN)
    for n, slab in enumerate(slabs):
        part = placed[n * COLS:(n + 1) * COLS]
        block = jnp.concatenate([part[:, g * 128:(g + 1) * 128] for g in range(4)], axis=0).T
        place = pl.ds(pl.multiple_of(slab * SLABS, SLABS), SLABS)
        for j in range(STEPS):
            out_ref[j // 5, place, (j % 5) * 128:(j % 5 + 1) * 128] = block[j * SLABS:(j + 1) * SLABS]
    o_ref[...] = jnp.swapaxes(out_ref[...], 0, 1).astype(jnp.bfloat16)


def params(mib):
    return pltpu.CompilerParams(vmem_limit_bytes=mib * 1024 * 1024)


def cost(rows, depth, columns):
    return pl.CostEstimate(flops=2 * max(rows, 256) * depth * columns, transcendentals=0,
                           bytes_accessed=2 * depth * columns)


def chunks():
    return jax.ShapeDtypeStruct((PAIRS, 2, HALF), jnp.bfloat16)


def pack(x, tab):
    return pl.pallas_call(
        pack_kernel, out_shape=(chunks(), like(tab)), in_specs=[ANY, ANY], out_specs=(VMEM, ANY),
        scratch_shapes=[pltpu.VMEM(x.shape, x.dtype), pltpu.VMEM(tab.shape, tab.dtype), pltpu.SemaphoreType.DMA((3,))],
        compiler_params=params(60), cost_estimate=cost(PAIRS * 4, SLAB, 2 * KP), name="pack")(x, tab)


def unpack(b):
    return pl.pallas_call(unpack_kernel, out_shape=jax.ShapeDtypeStruct((F, V, R, 4 * PAIRS), jnp.bfloat16),
                          in_specs=[VMEM], out_specs=VMEM, compiler_params=params(12), cost_estimate=cost(SLAB, PAIRS * 4, 2 * KP),
                          name="unpack")(b)


def coef(low, lev, gamma, beta, points, token):
    return pl.pallas_call(
        coef_kernel, out_shape=(jax.ShapeDtypeStruct((SLABS, 2, SLAB), jnp.float32),
                                jax.ShapeDtypeStruct((2, SLABS, 128), jnp.float32)),
        in_specs=[SMEM] * 4 + [VMEM, ANY], out_specs=(VMEM,) * 2, compiler_params=params(8),
        name="coef")(low, lev, gamma, beta, points, token)


def like(tab):
    return jax.ShapeDtypeStruct(tab.shape, tab.dtype)


def weigh(y, scale):
    return pl.pallas_call(
        weigh_kernel, out_shape=jax.ShapeDtypeStruct((SLABS, COLS, SLAB), jnp.bfloat16),
        in_specs=[VMEM, VMEM], out_specs=VMEM, compiler_params=params(8),
        cost_estimate=cost(SLABS * 128, SLAB, 128), name="weigh")(y, scale)


def pass_on(token, tab):
    return pl.pallas_call(pass_kernel, out_shape=like(tab), in_specs=[ANY, ANY], out_specs=ANY,
                          input_output_aliases={1: 0}, compiler_params=params(1), name="pass_on")(token, tab)


RAW = jax.ShapeDtypeStruct((COLS, KP), jnp.float32)


TURNED = jax.ShapeDtypeStruct((KP, SLAB), jnp.bfloat16)


def near(lev, w, tabs):
    return pl.pallas_call(
        near_kernel, out_shape=(RAW,) + (TURNED,) * NEARS, in_specs=[SMEM, VMEM] + [ANY] * NEARS,
        out_specs=(VMEM,) * (1 + NEARS),
        scratch_shapes=[pltpu.VMEM((NEARS, SLAB, KP), jnp.bfloat16), pltpu.SemaphoreType.DMA((NEARS,))],
        compiler_params=params(12), cost_estimate=pl.CostEstimate(flops=NEAR, bytes_accessed=0, transcendentals=0),
        name="near")(lev, w, *tabs)


def far(lev, w, raw, tabs):
    return pl.pallas_call(
        far_kernel, out_shape=(RAW,) + (TURNED,) * FARS, in_specs=[SMEM] + [VMEM] * (2 + FARS),
        out_specs=(VMEM,) * (1 + FARS),
        compiler_params=params(8), cost_estimate=cost(COLS, 4 * SLAB, KP), name="far")(lev, w, raw, *tabs)


def solve(low, lev, level, w, scale, raw, tabs):
    return pl.pallas_call(
        solve_kernel, out_shape=chunks(), in_specs=[SMEM] * 2 + [VMEM] * (4 + len(tabs)), out_specs=VMEM,
        scratch_shapes=[pltpu.VMEM((2, PAIRS, HALF), jnp.float32)],
        compiler_params=params(12), cost_estimate=cost(COLS, 9 * SLAB, KP),
        name="solve")(low, lev, level, w, scale, raw, *tabs)


def along_x(array, step):
    return lax.ppermute(array, "lev", [(d, (d + 2 * step * (1 - 2 * (d % 2))) % SLABS) for d in range(SLABS)])


def other_core(array):
    return lax.ppermute(array, "lev", [(d, d ^ 1) for d in range(SLABS)])


def local(fourier_in, table, points, pair_low, gamma, beta):
    lev = lax.axis_index("lev").astype(jnp.int32).reshape(1)
    own = jnp.swapaxes(table, 1, 2)[0]
    first = along_x(own, 1)
    sent, copied = pack(fourier_in, own)
    second = along_x(copied, -1)
    moved = lax.all_to_all(sent, "wave", split_axis=0, concat_axis=0, tiled=True)
    scale, level = coef(pair_low, lev, gamma, beta, points.reshape(1, NLAT), sent)
    first = pass_on(level, first)
    third = along_x(first, 1)
    second = pass_on(sent, second)
    cores = [other_core(tab) for tab in (copied, first, second)]
    weighted = weigh(moved, scale)
    raw, *tabs = near(lev, weighted, [own, first, second])
    third = pass_on(raw, third)
    last = other_core(third)
    raw, *more = far(lev, weighted, raw, cores + [third])
    tabs += more + [last]
    result = solve(pair_low, lev, level, weighted, scale, raw, tabs)
    back = lax.all_to_all(result, "wave", split_axis=0, concat_axis=0, tiled=True)
    return unpack(back)


def solution(mesh):
    placed = (P(None, "lev", "wave", None), P("wave", None, "lev"), P(), P("wave"), P(), P())
    return jax.shard_map(
        local, mesh=mesh, in_specs=placed, out_specs=P(None, "lev", "wave", None), check_vma=False
    )
```

```python
import jax
import jax.numpy as jnp
from jax import lax
from jax.experimental import pallas as pl
from jax.experimental.pallas import tpu as pltpu
from jax.sharding import PartitionSpec as P

F = 2
V = 4
R = 40
PAIRS = 64
SLABS = 8
SLAB = 320
KP = 1281
CUT = KP - 2
NLAT = 2560
STEPS = R // 4
COLS = 32
HALF = 640
NEAR = 75 * 10**8
NEARS = 3
FARS = 4

NT = (((1,), (1,)), ((), ()))
NN = (((1,), (0,)), ((), ()))
TN = (((0,), (0,)), ((), ()))
VMEM = pl.BlockSpec(memory_space=pltpu.VMEM)
ANY = pl.BlockSpec(memory_space=pl.ANY)
SMEM = pl.BlockSpec(memory_space=pltpu.SMEM)


def iota(shape, dim):
    return lax.broadcasted_iota(jnp.int32, shape, dim)


def ones_where(cond):
    return jnp.where(cond, 1.0, 0.0).astype(jnp.bfloat16)


def mul(a, b, dims):
    return lax.dot_general(a, b, dims, preferred_element_type=jnp.float32)


def by_member():
    row = iota((4 * PAIRS, 4 * PAIRS), 0)
    return ones_where(iota((4 * PAIRS, 4 * PAIRS), 1) == 4 * (row & (PAIRS - 1)) + (row >> 6))


def by_place():
    lane = iota((1, STEPS * 128), 1)
    source = ((lane >> 3) & 1) * V + ((lane >> 1) & 3)
    source = source * R + 4 * (lane >> 7) + ((lane >> 5) & 3)
    return ones_where(iota((F * V * R, STEPS * 128), 0) == source)


def lane_part(shape):
    lane = iota(shape, 1)
    return ((lane >> 4) & 1) * 2 + (lane & 1)


def pack_kernel(x_ref, tab_ref, o_ref, copy_ref, held_x, held_tab, sems):
    get_x = pltpu.make_async_copy(x_ref, held_x, sems.at[0])
    get_tab = pltpu.make_async_copy(tab_ref, held_tab, sems.at[1])
    put_tab = pltpu.make_async_copy(held_tab, copy_ref, sems.at[2])
    get_x.start()
    get_tab.start()
    get_x.wait()
    x = held_x[...].astype(jnp.float32).reshape(F * V * R, 4 * PAIRS).astype(jnp.bfloat16)
    turned = mul(by_member(), x, NT).astype(jnp.bfloat16)
    get_tab.wait()
    put_tab.start()
    placed = mul(turned, by_place(), NN)
    part = lane_part((PAIRS, STEPS * 128))
    out = placed[:PAIRS]
    for q in range(1, 4):
        out = jnp.where(part == q, placed[q * PAIRS:(q + 1) * PAIRS], out)
    halves = jnp.stack([out[:, :HALF], out[:, HALF:]], axis=0)
    o_ref[...] = jnp.swapaxes(halves, 0, 1).astype(jnp.bfloat16)
    put_tab.wait()


def unpack_kernel(b_ref, o_ref):
    b = jnp.swapaxes(b_ref[...].astype(jnp.float32), 0, 1)
    b = jnp.concatenate([b[0], b[1]], axis=1)
    part = lane_part((PAIRS, STEPS * 128))
    parts = [jnp.where(part == q, b, 0.0).astype(jnp.bfloat16) for q in range(4)]
    turned = mul(by_place(), jnp.concatenate(parts, axis=0), NT).astype(jnp.bfloat16)
    x = mul(turned, by_member(), NN)
    o_ref[...] = x.reshape(F, V, R, 4 * PAIRS).astype(jnp.bfloat16)


def spread_rows():
    row = iota((STEPS * SLABS, SLAB), 0)
    gap = iota((STEPS * SLABS, SLAB), 1) - (row & 7) * R - 4 * (row >> 3)
    return ones_where((gap >= 0) & (gap < 4))


def place_rows():
    lane = iota((1, 512), 1)
    row = (lane & 7) * R + 4 * ((lane >> 3) & 15) + (lane >> 7)
    return ones_where((iota((SLAB, 512), 0) == row) & (((lane >> 3) & 15) < STEPS))


def own_group():
    return (iota((4 * COLS, SLAB), 0) >> 5) == (iota((4 * COLS, SLAB), 1) & 3)


def coef_kernel(low_ref, lev_ref, gamma_ref, beta_ref, points_ref, scale_ref, level_ref):
    low = low_ref[0]
    points = jnp.concatenate([points_ref[:, s * SLAB:(s + 1) * SLAB] for s in range(SLABS)], axis=0)
    pts = points.astype(jnp.float32)
    weights = NLAT * pts / jnp.sum(pts)
    limit = jnp.minimum(CUT, (points >> 1) - 1)
    rows = jnp.stack([jnp.where(low <= limit, weights, 0.0), jnp.where(CUT - low <= limit, weights, 0.0)], axis=0)
    for s in range(SLABS):
        scale_ref[s] = rows[:, s, :]
    level = iota((SLABS, 128), 0) >> 1
    gval = jnp.zeros((SLABS, 128), jnp.float32)
    bval = jnp.zeros((SLABS, 128), jnp.float32)
    for v in range(V):
        gval = jnp.where(level == v, gamma_ref[lev_ref[0] * V + v], gval)
        bval = jnp.where(level == v, beta_ref[lev_ref[0] * V + v], bval)
    level_ref[0] = gval
    level_ref[1] = bval


def members(pair):
    return jnp.concatenate([jnp.broadcast_to(pair[m:m + 1], (COLS // 2, SLAB)) for m in range(2)], axis=0)


def weigh_kernel(y_ref, scale_ref, o_ref):
    spread = spread_rows()
    group = own_group()
    y = jnp.swapaxes(y_ref[...].astype(jnp.float32), 0, 1)
    for s in range(SLABS):
        rows = y[:, s * SLABS:(s + 1) * SLABS]
        block = jnp.concatenate([rows[j // 5, :, (j % 5) * 128:(j % 5 + 1) * 128] for j in range(STEPS)], axis=0)
        turned = jnp.where(group, mul(block.astype(jnp.bfloat16), spread, TN), 0.0)
        turned = turned[:32] + turned[32:64] + turned[64:96] + turned[96:]
        o_ref[s] = (turned * members(scale_ref[s])).astype(jnp.bfloat16)


def slab_order(lev):
    way = 2 - 4 * (lev & 1)
    behind, ahead, far = (lev - way) & 7, (lev + way) & 7, lev ^ 4
    return [lev, behind, ahead, lev ^ 1, ahead ^ 1, behind ^ 1, far, far ^ 1]


def add_up(raw, w_ref, slabs, tabs):
    for slab, tab in zip(slabs, tabs):
        term = mul(w_ref[slab], tab[...], NN)
        raw = term if raw is None else raw + term
    return raw


def near_kernel(lev_ref, w_ref, *refs):
    tabs, raw_ref, turned, held, sems = refs[:NEARS], refs[NEARS], refs[NEARS + 1:-2], *refs[-2:]
    copies = [pltpu.make_async_copy(tabs[n], held.at[n], sems.at[n]) for n in range(NEARS)]
    for copy in copies:
        copy.start()
    slabs = slab_order(lev_ref[0])
    raw = None
    for n in range(NEARS):
        copies[n].wait()
        raw = add_up(raw, w_ref, slabs[n:n + 1], [held.at[n]])
        turned[n][...] = held[n].T
    raw_ref[...] = raw


def far_kernel(lev_ref, w_ref, raw_ref, *refs):
    tabs, total_ref, turned = refs[:FARS], refs[FARS], refs[FARS + 1:]
    total_ref[...] = add_up(raw_ref[...], w_ref, slab_order(lev_ref[0])[NEARS:], tabs)
    for tab, turn in zip(tabs, turned):
        turn[...] = tab[...].T


def pass_kernel(token_ref, tab_ref, same_ref):
    pass


def solve_kernel(low_ref, lev_ref, level_ref, w_ref, scale_ref, raw_ref, *refs):
    *tabs, o_ref, out_ref = refs
    low = low_ref[0]
    slabs = slab_order(lev_ref[0])
    wide = add_up(raw_ref[...], w_ref, slabs[7:], tabs[7:])
    kidx = iota((1, KP), 1)
    first = kidx <= CUT - low
    degree = jnp.where(first, low + kidx, kidx - 1).astype(jnp.float32)
    eig = degree * (degree + 1.0) / (CUT * (CUT + 1.0))
    gval = level_ref[0, :, 0:1]
    bval = level_ref[1, :, 0:1]
    spectra = jnp.where(first, wide[:16], wide[16:])
    drive, mass = spectra[:8], spectra[8:]
    solved = (drive - bval * eig * mass) / (1.0 + gval * eig)
    spec = jnp.concatenate([solved, mass + bval * solved], axis=0)
    expanded = jnp.concatenate([jnp.where(first, spec, 0.0), jnp.where(first, 0.0, spec)], axis=0).astype(jnp.bfloat16)
    rows = []
    for n, slab in enumerate(slabs):
        part = mul(expanded, tabs[n][...], NN if n < NEARS + FARS else NT)
        rows.append(jnp.where(members(scale_ref[slab]) > 0.0, part, 0.0).astype(jnp.bfloat16))
    placed = mul(jnp.concatenate(rows, axis=0), place_rows(), NN)
    for n, slab in enumerate(slabs):
        part = placed[n * COLS:(n + 1) * COLS]
        block = jnp.concatenate([part[:, g * 128:(g + 1) * 128] for g in range(4)], axis=0).T
        place = pl.ds(pl.multiple_of(slab * SLABS, SLABS), SLABS)
        for j in range(STEPS):
            out_ref[j // 5, place, (j % 5) * 128:(j % 5 + 1) * 128] = block[j * SLABS:(j + 1) * SLABS]
    o_ref[...] = jnp.swapaxes(out_ref[...], 0, 1).astype(jnp.bfloat16)


def params(mib):
    return pltpu.CompilerParams(vmem_limit_bytes=mib * 1024 * 1024)


def cost(rows, depth, columns):
    return pl.CostEstimate(flops=2 * max(rows, 256) * depth * columns, transcendentals=0,
                           bytes_accessed=2 * depth * columns)


def chunks():
    return jax.ShapeDtypeStruct((PAIRS, 2, HALF), jnp.bfloat16)


def pack(x, tab):
    return pl.pallas_call(
        pack_kernel, out_shape=(chunks(), like(tab)), in_specs=[ANY, ANY], out_specs=(VMEM, ANY),
        scratch_shapes=[pltpu.VMEM(x.shape, x.dtype), pltpu.VMEM(tab.shape, tab.dtype), pltpu.SemaphoreType.DMA((3,))],
        compiler_params=params(60), cost_estimate=cost(PAIRS * 4, SLAB, 2 * KP), name="pack")(x, tab)


def unpack(b):
    return pl.pallas_call(unpack_kernel, out_shape=jax.ShapeDtypeStruct((F, V, R, 4 * PAIRS), jnp.bfloat16),
                          in_specs=[VMEM], out_specs=VMEM, compiler_params=params(12), cost_estimate=cost(SLAB, PAIRS * 4, 2 * KP),
                          name="unpack")(b)


def coef(low, lev, gamma, beta, points):
    return pl.pallas_call(
        coef_kernel, out_shape=(jax.ShapeDtypeStruct((SLABS, 2, SLAB), jnp.float32),
                                jax.ShapeDtypeStruct((2, SLABS, 128), jnp.float32)),
        in_specs=[SMEM] * 4 + [VMEM], out_specs=(VMEM,) * 2, compiler_params=params(8),
        name="coef")(low, lev, gamma, beta, points)


def like(tab):
    return jax.ShapeDtypeStruct(tab.shape, tab.dtype)


def weigh(y, scale):
    return pl.pallas_call(
        weigh_kernel, out_shape=jax.ShapeDtypeStruct((SLABS, COLS, SLAB), jnp.bfloat16),
        in_specs=[VMEM, VMEM], out_specs=VMEM, compiler_params=params(8),
        cost_estimate=cost(SLABS * 128, SLAB, 128), name="weigh")(y, scale)


def pass_on(token, tab):
    return pl.pallas_call(pass_kernel, out_shape=like(tab), in_specs=[ANY, ANY], out_specs=ANY,
                          input_output_aliases={1: 0}, compiler_params=params(1), name="pass_on")(token, tab)


RAW = jax.ShapeDtypeStruct((COLS, KP), jnp.float32)


TURNED = jax.ShapeDtypeStruct((KP, SLAB), jnp.bfloat16)


def near(lev, w, tabs):
    return pl.pallas_call(
        near_kernel, out_shape=(RAW,) + (TURNED,) * NEARS, in_specs=[SMEM, VMEM] + [ANY] * NEARS,
        out_specs=(VMEM,) * (1 + NEARS),
        scratch_shapes=[pltpu.VMEM((NEARS, SLAB, KP), jnp.bfloat16), pltpu.SemaphoreType.DMA((NEARS,))],
        compiler_params=params(12), cost_estimate=pl.CostEstimate(flops=NEAR, bytes_accessed=0, transcendentals=0),
        name="near")(lev, w, *tabs)


def far(lev, w, raw, tabs):
    return pl.pallas_call(
        far_kernel, out_shape=(RAW,) + (TURNED,) * FARS, in_specs=[SMEM] + [VMEM] * (2 + FARS),
        out_specs=(VMEM,) * (1 + FARS),
        compiler_params=params(8), cost_estimate=cost(COLS, 4 * SLAB, KP), name="far")(lev, w, raw, *tabs)


def solve(low, lev, level, w, scale, raw, tabs):
    return pl.pallas_call(
        solve_kernel, out_shape=chunks(), in_specs=[SMEM] * 2 + [VMEM] * (4 + len(tabs)), out_specs=VMEM,
        scratch_shapes=[pltpu.VMEM((2, PAIRS, HALF), jnp.float32)],
        compiler_params=params(12), cost_estimate=cost(COLS, 9 * SLAB, KP),
        name="solve")(low, lev, level, w, scale, raw, *tabs)


def along_x(array, step):
    return lax.ppermute(array, "lev", [(d, (d + 2 * step * (1 - 2 * (d % 2))) % SLABS) for d in range(SLABS)])


def other_core(array):
    return lax.ppermute(array, "lev", [(d, d ^ 1) for d in range(SLABS)])


def local(fourier_in, table, points, pair_low, gamma, beta):
    lev = lax.axis_index("lev").astype(jnp.int32).reshape(1)
    own = jnp.swapaxes(table, 1, 2)[0]
    first = along_x(own, 1)
    sent, copied = pack(fourier_in, own)
    second = along_x(copied, -1)
    moved = lax.all_to_all(sent, "wave", split_axis=0, concat_axis=0, tiled=True)
    scale, level = coef(pair_low, lev, gamma, beta, points.reshape(1, NLAT))
    first = pass_on(sent, first)
    third = along_x(first, 1)
    second = pass_on(sent, second)
    cores = [other_core(tab) for tab in (copied, first, second)]
    weighted = weigh(moved, scale)
    raw, *tabs = near(lev, weighted, [own, first, second])
    third = pass_on(raw, third)
    last = other_core(third)
    raw, *more = far(lev, weighted, raw, cores + [third])
    tabs += more + [last]
    result = solve(pair_low, lev, level, weighted, scale, raw, tabs)
    back = lax.all_to_all(result, "wave", split_axis=0, concat_axis=0, tiled=True)
    return unpack(back)


def solution(mesh):
    placed = (P(None, "lev", "wave", None), P("wave", None, "lev"), P(), P("wave"), P(), P())
    return jax.shard_map(
        local, mesh=mesh, in_specs=placed, out_specs=P(None, "lev", "wave", None), check_vma=False
    )
```

```python
import jax
import jax.numpy as jnp
from jax import lax
from jax.experimental import pallas as pl
from jax.experimental.pallas import tpu as pltpu
from jax.sharding import PartitionSpec as P

F = 2
V = 4
R = 40
PAIRS = 64
SLABS = 8
SLAB = 320
KP = 1281
CUT = KP - 2
NLAT = 2560
STEPS = R // 4
COLS = 32
HALF = 640
NEAR = 75 * 10**8
NEARS = 3
FARS = 4

NT = (((1,), (1,)), ((), ()))
NN = (((1,), (0,)), ((), ()))
TN = (((0,), (0,)), ((), ()))
VMEM = pl.BlockSpec(memory_space=pltpu.VMEM)
ANY = pl.BlockSpec(memory_space=pl.ANY)
SMEM = pl.BlockSpec(memory_space=pltpu.SMEM)


def iota(shape, dim):
    return lax.broadcasted_iota(jnp.int32, shape, dim)


def ones_where(cond):
    return jnp.where(cond, 1.0, 0.0).astype(jnp.bfloat16)


def mul(a, b, dims):
    return lax.dot_general(a, b, dims, preferred_element_type=jnp.float32)


def by_member():
    row = iota((4 * PAIRS, 4 * PAIRS), 0)
    return ones_where(iota((4 * PAIRS, 4 * PAIRS), 1) == 4 * (row & (PAIRS - 1)) + (row >> 6))


def by_place():
    lane = iota((1, STEPS * 128), 1)
    source = ((lane >> 3) & 1) * V + ((lane >> 1) & 3)
    source = source * R + 4 * (lane >> 7) + ((lane >> 5) & 3)
    return ones_where(iota((F * V * R, STEPS * 128), 0) == source)


def lane_part(shape):
    lane = iota(shape, 1)
    return ((lane >> 4) & 1) * 2 + (lane & 1)


def pack_kernel(x_ref, tab_ref, o_ref, copy_ref, held_x, held_tab, sems):
    get_x = pltpu.make_async_copy(x_ref, held_x, sems.at[0])
    get_tab = pltpu.make_async_copy(tab_ref, held_tab, sems.at[1])
    put_tab = pltpu.make_async_copy(held_tab, copy_ref, sems.at[2])
    get_x.start()
    get_tab.start()
    member, place = by_member(), by_place()
    get_x.wait()
    x = held_x[...].astype(jnp.float32).reshape(F * V * R, 4 * PAIRS).astype(jnp.bfloat16)
    turned = mul(member, x, NT).astype(jnp.bfloat16)
    get_tab.wait()
    put_tab.start()
    placed = mul(turned, place, NN)
    part = lane_part((PAIRS, STEPS * 128))
    out = placed[:PAIRS]
    for q in range(1, 4):
        out = jnp.where(part == q, placed[q * PAIRS:(q + 1) * PAIRS], out)
    halves = jnp.stack([out[:, :HALF], out[:, HALF:]], axis=0)
    o_ref[...] = jnp.swapaxes(halves, 0, 1).astype(jnp.bfloat16)
    put_tab.wait()


def unpack_kernel(b_ref, place_ref, member_ref, o_ref):
    b = jnp.swapaxes(b_ref[...].astype(jnp.float32), 0, 1)
    b = jnp.concatenate([b[0], b[1]], axis=1)
    part = lane_part((PAIRS, STEPS * 128))
    parts = [jnp.where(part == q, b, 0.0).astype(jnp.bfloat16) for q in range(4)]
    turned = mul(place_ref[...], jnp.concatenate(parts, axis=0), NT).astype(jnp.bfloat16)
    x = mul(turned, member_ref[...], NN)
    o_ref[...] = x.reshape(F, V, R, 4 * PAIRS).astype(jnp.bfloat16)


def spread_rows():
    row = iota((STEPS * SLABS, SLAB), 0)
    gap = iota((STEPS * SLABS, SLAB), 1) - (row & 7) * R - 4 * (row >> 3)
    return ones_where((gap >= 0) & (gap < 4))


def place_rows():
    lane = iota((1, 512), 1)
    row = (lane & 7) * R + 4 * ((lane >> 3) & 15) + (lane >> 7)
    return ones_where((iota((SLAB, 512), 0) == row) & (((lane >> 3) & 15) < STEPS))


def own_group():
    return (iota((4 * COLS, SLAB), 0) >> 5) == (iota((4 * COLS, SLAB), 1) & 3)


def coef_kernel(low_ref, lev_ref, gamma_ref, beta_ref, points_ref, scale_ref, level_ref):
    low = low_ref[0]
    points = jnp.concatenate([points_ref[:, s * SLAB:(s + 1) * SLAB] for s in range(SLABS)], axis=0)
    pts = points.astype(jnp.float32)
    weights = NLAT * pts / jnp.sum(pts)
    limit = jnp.minimum(CUT, (points >> 1) - 1)
    rows = jnp.stack([jnp.where(low <= limit, weights, 0.0), jnp.where(CUT - low <= limit, weights, 0.0)], axis=0)
    for s in range(SLABS):
        scale_ref[s] = rows[:, s, :]
    level = iota((SLABS, 128), 0) >> 1
    gval = jnp.zeros((SLABS, 128), jnp.float32)
    bval = jnp.zeros((SLABS, 128), jnp.float32)
    for v in range(V):
        gval = jnp.where(level == v, gamma_ref[lev_ref[0] * V + v], gval)
        bval = jnp.where(level == v, beta_ref[lev_ref[0] * V + v], bval)
    level_ref[0] = gval
    level_ref[1] = bval


def members(pair):
    return jnp.concatenate([jnp.broadcast_to(pair[m:m + 1], (COLS // 2, SLAB)) for m in range(2)], axis=0)


def weigh_kernel(y_ref, scale_ref, o_ref):
    spread = spread_rows()
    group = own_group()
    y = jnp.swapaxes(y_ref[...].astype(jnp.float32), 0, 1)
    for s in range(SLABS):
        rows = y[:, s * SLABS:(s + 1) * SLABS]
        block = jnp.concatenate([rows[j // 5, :, (j % 5) * 128:(j % 5 + 1) * 128] for j in range(STEPS)], axis=0)
        turned = jnp.where(group, mul(block.astype(jnp.bfloat16), spread, TN), 0.0)
        turned = turned[:32] + turned[32:64] + turned[64:96] + turned[96:]
        o_ref[s] = (turned * members(scale_ref[s])).astype(jnp.bfloat16)


def slab_order(lev):
    way = 2 - 4 * (lev & 1)
    behind, ahead, far = (lev - way) & 7, (lev + way) & 7, lev ^ 4
    return [lev, behind, ahead, lev ^ 1, ahead ^ 1, behind ^ 1, far, far ^ 1]


def add_up(raw, w_ref, slabs, tabs):
    for slab, tab in zip(slabs, tabs):
        term = mul(w_ref[slab], tab[...], NN)
        raw = term if raw is None else raw + term
    return raw


def near_kernel(lev_ref, w_ref, *refs):
    tabs, raw_ref, turned, held, sems = refs[:NEARS], refs[NEARS], refs[NEARS + 1:-2], *refs[-2:]
    copies = [pltpu.make_async_copy(tabs[n], held.at[n], sems.at[n]) for n in range(NEARS)]
    for copy in copies:
        copy.start()
    slabs = slab_order(lev_ref[0])
    raw = None
    for n in range(NEARS):
        copies[n].wait()
        raw = add_up(raw, w_ref, slabs[n:n + 1], [held.at[n]])
        turned[n][...] = held[n].T
    raw_ref[...] = raw


def far_kernel(lev_ref, w_ref, raw_ref, *refs):
    tabs, total_ref, turned, made = refs[:FARS], refs[FARS], refs[FARS + 1:-3], refs[-3:]
    total_ref[...] = add_up(raw_ref[...], w_ref, slab_order(lev_ref[0])[NEARS:], tabs)
    for tab, turn in zip(tabs, turned):
        turn[...] = tab[...].T
    for made_ref, make in zip(made, (by_place, by_member, place_rows)):
        made_ref[...] = make()


def pass_kernel(token_ref, tab_ref, same_ref):
    pass


def solve_kernel(low_ref, lev_ref, level_ref, w_ref, scale_ref, raw_ref, rows_ref, *refs):
    *tabs, o_ref, out_ref = refs
    low = low_ref[0]
    slabs = slab_order(lev_ref[0])
    wide = add_up(raw_ref[...], w_ref, slabs[7:], tabs[7:])
    kidx = iota((1, KP), 1)
    first = kidx <= CUT - low
    degree = jnp.where(first, low + kidx, kidx - 1).astype(jnp.float32)
    eig = degree * (degree + 1.0) / (CUT * (CUT + 1.0))
    gval = level_ref[0, :, 0:1]
    bval = level_ref[1, :, 0:1]
    spectra = jnp.where(first, wide[:16], wide[16:])
    drive, mass = spectra[:8], spectra[8:]
    solved = (drive - bval * eig * mass) / (1.0 + gval * eig)
    spec = jnp.concatenate([solved, mass + bval * solved], axis=0)
    expanded = jnp.concatenate([jnp.where(first, spec, 0.0), jnp.where(first, 0.0, spec)], axis=0).astype(jnp.bfloat16)
    rows = []
    for n, slab in enumerate(slabs):
        part = mul(expanded, tabs[n][...], NN if n < NEARS + FARS else NT)
        rows.append(jnp.where(members(scale_ref[slab]) > 0.0, part, 0.0).astype(jnp.bfloat16))
    placed = mul(jnp.concatenate(rows, axis=0), rows_ref[...], NN)
    for n, slab in enumerate(slabs):
        part = placed[n * COLS:(n + 1) * COLS]
        block = jnp.concatenate([part[:, g * 128:(g + 1) * 128] for g in range(4)], axis=0).T
        place = pl.ds(pl.multiple_of(slab * SLABS, SLABS), SLABS)
        for j in range(STEPS):
            out_ref[j // 5, place, (j % 5) * 128:(j % 5 + 1) * 128] = block[j * SLABS:(j + 1) * SLABS]
    o_ref[...] = jnp.swapaxes(out_ref[...], 0, 1).astype(jnp.bfloat16)


def params(mib):
    return pltpu.CompilerParams(vmem_limit_bytes=mib * 1024 * 1024)


def cost(rows, depth, columns):
    return pl.CostEstimate(flops=2 * max(rows, 256) * depth * columns, transcendentals=0,
                           bytes_accessed=2 * depth * columns)


def chunks():
    return jax.ShapeDtypeStruct((PAIRS, 2, HALF), jnp.bfloat16)


def pack(x, tab):
    return pl.pallas_call(
        pack_kernel, out_shape=(chunks(), like(tab)), in_specs=[ANY, ANY], out_specs=(VMEM, ANY),
        scratch_shapes=[pltpu.VMEM(x.shape, x.dtype), pltpu.VMEM(tab.shape, tab.dtype), pltpu.SemaphoreType.DMA((3,))],
        compiler_params=params(60), cost_estimate=cost(PAIRS * 4, SLAB, 2 * KP), name="pack")(x, tab)


def unpack(b, place, member):
    return pl.pallas_call(unpack_kernel, out_shape=jax.ShapeDtypeStruct((F, V, R, 4 * PAIRS), jnp.bfloat16),
                          in_specs=[VMEM] * 3, out_specs=VMEM, compiler_params=params(12),
                          cost_estimate=cost(SLAB, PAIRS * 4, 2 * KP), name="unpack")(b, place, member)


def coef(low, lev, gamma, beta, points):
    return pl.pallas_call(
        coef_kernel, out_shape=(jax.ShapeDtypeStruct((SLABS, 2, SLAB), jnp.float32),
                                jax.ShapeDtypeStruct((2, SLABS, 128), jnp.float32)),
        in_specs=[SMEM] * 4 + [VMEM], out_specs=(VMEM,) * 2, compiler_params=params(8),
        name="coef")(low, lev, gamma, beta, points)


def like(tab):
    return jax.ShapeDtypeStruct(tab.shape, tab.dtype)


def weigh(y, scale):
    return pl.pallas_call(
        weigh_kernel, out_shape=jax.ShapeDtypeStruct((SLABS, COLS, SLAB), jnp.bfloat16),
        in_specs=[VMEM, VMEM], out_specs=VMEM, compiler_params=params(8),
        cost_estimate=cost(SLABS * 128, SLAB, 128), name="weigh")(y, scale)


def pass_on(token, tab):
    return pl.pallas_call(pass_kernel, out_shape=like(tab), in_specs=[ANY, ANY], out_specs=ANY,
                          input_output_aliases={1: 0}, compiler_params=params(1), name="pass_on")(token, tab)


RAW = jax.ShapeDtypeStruct((COLS, KP), jnp.float32)


MADE = tuple(jax.ShapeDtypeStruct(shape, jnp.bfloat16)
             for shape in ((F * V * R, STEPS * 128), (4 * PAIRS, 4 * PAIRS), (SLAB, 512)))
TURNED = jax.ShapeDtypeStruct((KP, SLAB), jnp.bfloat16)


def near(lev, w, tabs):
    return pl.pallas_call(
        near_kernel, out_shape=(RAW,) + (TURNED,) * NEARS, in_specs=[SMEM, VMEM] + [ANY] * NEARS,
        out_specs=(VMEM,) * (1 + NEARS),
        scratch_shapes=[pltpu.VMEM((NEARS, SLAB, KP), jnp.bfloat16), pltpu.SemaphoreType.DMA((NEARS,))],
        compiler_params=params(12), cost_estimate=pl.CostEstimate(flops=NEAR, bytes_accessed=0, transcendentals=0),
        name="near")(lev, w, *tabs)


def far(lev, w, raw, tabs):
    return pl.pallas_call(
        far_kernel, out_shape=(RAW,) + (TURNED,) * FARS + MADE, in_specs=[SMEM] + [VMEM] * (2 + FARS),
        out_specs=(VMEM,) * (4 + FARS),
        compiler_params=params(8), cost_estimate=cost(COLS, 4 * SLAB, KP), name="far")(lev, w, raw, *tabs)


def solve(low, lev, level, w, scale, raw, rows, tabs):
    return pl.pallas_call(
        solve_kernel, out_shape=chunks(), in_specs=[SMEM] * 2 + [VMEM] * (5 + len(tabs)), out_specs=VMEM,
        scratch_shapes=[pltpu.VMEM((2, PAIRS, HALF), jnp.float32)],
        compiler_params=params(12), cost_estimate=cost(COLS, 9 * SLAB, KP),
        name="solve")(low, lev, level, w, scale, raw, rows, *tabs)


def along_x(array, step):
    return lax.ppermute(array, "lev", [(d, (d + 2 * step * (1 - 2 * (d % 2))) % SLABS) for d in range(SLABS)])


def other_core(array):
    return lax.ppermute(array, "lev", [(d, d ^ 1) for d in range(SLABS)])


def local(fourier_in, table, points, pair_low, gamma, beta):
    lev = lax.axis_index("lev").astype(jnp.int32).reshape(1)
    own = jnp.swapaxes(table, 1, 2)[0]
    first = along_x(own, 1)
    sent, copied = pack(fourier_in, own)
    second = along_x(copied, -1)
    moved = lax.all_to_all(sent, "wave", split_axis=0, concat_axis=0, tiled=True)
    scale, level = coef(pair_low, lev, gamma, beta, points.reshape(1, NLAT))
    first = pass_on(sent, first)
    third = along_x(first, 1)
    second = pass_on(sent, second)
    cores = [other_core(tab) for tab in (copied, first, second)]
    weighted = weigh(moved, scale)
    raw, *tabs = near(lev, weighted, [own, first, second])
    third = pass_on(raw, third)
    last = other_core(third)
    raw, *more, place, member, rows = far(lev, weighted, raw, cores + [third])
    tabs += more + [last]
    result = solve(pair_low, lev, level, weighted, scale, raw, rows, tabs)
    back = lax.all_to_all(result, "wave", split_axis=0, concat_axis=0, tiled=True)
    return unpack(back, place, member)


def solution(mesh):
    placed = (P(None, "lev", "wave", None), P("wave", None, "lev"), P(), P("wave"), P(), P())
    return jax.shard_map(
        local, mesh=mesh, in_specs=placed, out_specs=P(None, "lev", "wave", None), check_vma=False
    )
```

```python
import jax
import jax.numpy as jnp
from jax import lax
from jax.experimental import pallas as pl
from jax.experimental.pallas import tpu as pltpu
from jax.sharding import PartitionSpec as P

F = 2
V = 4
R = 40
PAIRS = 64
SLABS = 8
SLAB = 320
KP = 1281
CUT = KP - 2
NLAT = 2560
STEPS = R // 4
COLS = 32
HALF = 640
NEAR = 73 * 10**8
NEARS = 3
FARS = 4

NT = (((1,), (1,)), ((), ()))
NN = (((1,), (0,)), ((), ()))
TN = (((0,), (0,)), ((), ()))
VMEM = pl.BlockSpec(memory_space=pltpu.VMEM)
ANY = pl.BlockSpec(memory_space=pl.ANY)
SMEM = pl.BlockSpec(memory_space=pltpu.SMEM)


def iota(shape, dim):
    return lax.broadcasted_iota(jnp.int32, shape, dim)


def ones_where(cond):
    return jnp.where(cond, 1.0, 0.0).astype(jnp.bfloat16)


def mul(a, b, dims):
    return lax.dot_general(a, b, dims, preferred_element_type=jnp.float32)


def by_member():
    row = iota((4 * PAIRS, 4 * PAIRS), 0)
    return ones_where(iota((4 * PAIRS, 4 * PAIRS), 1) == 4 * (row & (PAIRS - 1)) + (row >> 6))


def by_place():
    lane = iota((1, STEPS * 128), 1)
    source = ((lane >> 3) & 1) * V + ((lane >> 1) & 3)
    source = source * R + 4 * (lane >> 7) + ((lane >> 5) & 3)
    return ones_where(iota((F * V * R, STEPS * 128), 0) == source)


def lane_part(shape):
    lane = iota(shape, 1)
    return ((lane >> 4) & 1) * 2 + (lane & 1)


def pack_kernel(x_ref, tab_ref, o_ref, copy_ref, held_x, held_tab, sems):
    get_x = pltpu.make_async_copy(x_ref, held_x, sems.at[0])
    get_tab = pltpu.make_async_copy(tab_ref, held_tab, sems.at[1])
    put_tab = pltpu.make_async_copy(held_tab, copy_ref, sems.at[2])
    get_x.start()
    get_tab.start()
    get_x.wait()
    x = held_x[...].astype(jnp.float32).reshape(F * V * R, 4 * PAIRS).astype(jnp.bfloat16)
    turned = mul(by_member(), x, NT).astype(jnp.bfloat16)
    get_tab.wait()
    put_tab.start()
    placed = mul(turned, by_place(), NN)
    part = lane_part((PAIRS, STEPS * 128))
    out = placed[:PAIRS]
    for q in range(1, 4):
        out = jnp.where(part == q, placed[q * PAIRS:(q + 1) * PAIRS], out)
    halves = jnp.stack([out[:, :HALF], out[:, HALF:]], axis=0)
    o_ref[...] = jnp.swapaxes(halves, 0, 1).astype(jnp.bfloat16)
    put_tab.wait()


def unpack_kernel(b_ref, o_ref):
    b = jnp.swapaxes(b_ref[...].astype(jnp.float32), 0, 1)
    b = jnp.concatenate([b[0], b[1]], axis=1)
    part = lane_part((PAIRS, STEPS * 128))
    parts = [jnp.where(part == q, b, 0.0).astype(jnp.bfloat16) for q in range(4)]
    turned = mul(by_place(), jnp.concatenate(parts, axis=0), NT).astype(jnp.bfloat16)
    x = mul(turned, by_member(), NN)
    o_ref[...] = x.reshape(F, V, R, 4 * PAIRS).astype(jnp.bfloat16)


def spread_rows():
    row = iota((STEPS * SLABS, SLAB), 0)
    gap = iota((STEPS * SLABS, SLAB), 1) - (row & 7) * R - 4 * (row >> 3)
    return ones_where((gap >= 0) & (gap < 4))


def place_rows():
    lane = iota((1, 512), 1)
    row = (lane & 7) * R + 4 * ((lane >> 3) & 15) + (lane >> 7)
    return ones_where((iota((SLAB, 512), 0) == row) & (((lane >> 3) & 15) < STEPS))


def own_group():
    return (iota((4 * COLS, SLAB), 0) >> 5) == (iota((4 * COLS, SLAB), 1) & 3)


def coef_kernel(low_ref, lev_ref, gamma_ref, beta_ref, points_ref, scale_ref, level_ref):
    low = low_ref[0]
    points = jnp.concatenate([points_ref[:, s * SLAB:(s + 1) * SLAB] for s in range(SLABS)], axis=0)
    pts = points.astype(jnp.float32)
    weights = NLAT * pts / jnp.sum(pts)
    limit = jnp.minimum(CUT, (points >> 1) - 1)
    rows = jnp.stack([jnp.where(low <= limit, weights, 0.0), jnp.where(CUT - low <= limit, weights, 0.0)], axis=0)
    for s in range(SLABS):
        scale_ref[s] = rows[:, s, :]
    level = iota((SLABS, 128), 0) >> 1
    gval = jnp.zeros((SLABS, 128), jnp.float32)
    bval = jnp.zeros((SLABS, 128), jnp.float32)
    for v in range(V):
        gval = jnp.where(level == v, gamma_ref[lev_ref[0] * V + v], gval)
        bval = jnp.where(level == v, beta_ref[lev_ref[0] * V + v], bval)
    level_ref[0] = gval
    level_ref[1] = bval


def members(pair):
    return jnp.concatenate([jnp.broadcast_to(pair[m:m + 1], (COLS // 2, SLAB)) for m in range(2)], axis=0)


def weigh_kernel(y_ref, scale_ref, o_ref):
    spread = spread_rows()
    group = own_group()
    y = jnp.swapaxes(y_ref[...].astype(jnp.float32), 0, 1)
    for s in range(SLABS):
        rows = y[:, s * SLABS:(s + 1) * SLABS]
        block = jnp.concatenate([rows[j // 5, :, (j % 5) * 128:(j % 5 + 1) * 128] for j in range(STEPS)], axis=0)
        turned = jnp.where(group, mul(block.astype(jnp.bfloat16), spread, TN), 0.0)
        turned = turned[:32] + turned[32:64] + turned[64:96] + turned[96:]
        o_ref[s] = (turned * members(scale_ref[s])).astype(jnp.bfloat16)


def slab_order(lev):
    way = 2 - 4 * (lev & 1)
    behind, ahead, far = (lev - way) & 7, (lev + way) & 7, lev ^ 4
    return [lev, behind, ahead, lev ^ 1, ahead ^ 1, behind ^ 1, far, far ^ 1]


def add_up(raw, w_ref, slabs, tabs):
    for slab, tab in zip(slabs, tabs):
        term = mul(w_ref[slab], tab[...], NN)
        raw = term if raw is None else raw + term
    return raw


def near_kernel(lev_ref, w_ref, *refs):
    tabs, raw_ref, turned, same_ref, held, sems = refs[:NEARS], refs[NEARS], refs[NEARS + 1:-3], *refs[-3:]
    places = [same_ref] + [held.at[n] for n in range(NEARS - 1)]
    copies = [pltpu.make_async_copy(tabs[n], places[n], sems.at[n]) for n in range(NEARS)]
    for copy in copies:
        copy.start()
    slabs = slab_order(lev_ref[0])
    raw = None
    for n in range(NEARS):
        copies[n].wait()
        raw = add_up(raw, w_ref, slabs[n:n + 1], places[n:n + 1])
        turned[n][...] = places[n][...].T
    raw_ref[...] = raw


def far_kernel(lev_ref, w_ref, raw_ref, *refs):
    tabs, total_ref, turned = refs[:FARS], refs[FARS], refs[FARS + 1:]
    total_ref[...] = add_up(raw_ref[...], w_ref, slab_order(lev_ref[0])[NEARS:], tabs)
    for tab, turn in zip(tabs, turned):
        turn[...] = tab[...].T


def pass_kernel(token_ref, tab_ref, same_ref):
    pass


def solve_kernel(low_ref, lev_ref, level_ref, w_ref, scale_ref, raw_ref, *refs):
    *tabs, o_ref, out_ref = refs
    low = low_ref[0]
    slabs = slab_order(lev_ref[0])
    wide = add_up(raw_ref[...], w_ref, slabs[7:], tabs[7:])
    kidx = iota((1, KP), 1)
    first = kidx <= CUT - low
    degree = jnp.where(first, low + kidx, kidx - 1).astype(jnp.float32)
    eig = degree * (degree + 1.0) / (CUT * (CUT + 1.0))
    gval = level_ref[0, :, 0:1]
    bval = level_ref[1, :, 0:1]
    spectra = jnp.where(first, wide[:16], wide[16:])
    drive, mass = spectra[:8], spectra[8:]
    solved = (drive - bval * eig * mass) / (1.0 + gval * eig)
    spec = jnp.concatenate([solved, mass + bval * solved], axis=0)
    expanded = jnp.concatenate([jnp.where(first, spec, 0.0), jnp.where(first, 0.0, spec)], axis=0).astype(jnp.bfloat16)
    rows = []
    for n, slab in enumerate(slabs):
        part = mul(expanded, tabs[n][...], NN if n < NEARS + FARS else NT)
        rows.append(jnp.where(members(scale_ref[slab]) > 0.0, part, 0.0).astype(jnp.bfloat16))
    placed = mul(jnp.concatenate(rows, axis=0), place_rows(), NN)
    for n, slab in enumerate(slabs):
        part = placed[n * COLS:(n + 1) * COLS]
        block = jnp.concatenate([part[:, g * 128:(g + 1) * 128] for g in range(4)], axis=0).T
        place = pl.ds(pl.multiple_of(slab * SLABS, SLABS), SLABS)
        for j in range(STEPS):
            out_ref[j // 5, place, (j % 5) * 128:(j % 5 + 1) * 128] = block[j * SLABS:(j + 1) * SLABS]
    o_ref[...] = jnp.swapaxes(out_ref[...], 0, 1).astype(jnp.bfloat16)


def params(mib):
    return pltpu.CompilerParams(vmem_limit_bytes=mib * 1024 * 1024)


def cost(rows, depth, columns):
    return pl.CostEstimate(flops=2 * max(rows, 256) * depth * columns, transcendentals=0,
                           bytes_accessed=2 * depth * columns)


def chunks():
    return jax.ShapeDtypeStruct((PAIRS, 2, HALF), jnp.bfloat16)


def pack(x, tab):
    return pl.pallas_call(
        pack_kernel, out_shape=(chunks(), like(tab)), in_specs=[ANY, ANY], out_specs=(VMEM, ANY),
        scratch_shapes=[pltpu.VMEM(x.shape, x.dtype), pltpu.VMEM(tab.shape, tab.dtype), pltpu.SemaphoreType.DMA((3,))],
        compiler_params=params(60), cost_estimate=cost(PAIRS * 4, SLAB, 2 * KP), name="pack")(x, tab)


def unpack(b):
    return pl.pallas_call(unpack_kernel, out_shape=jax.ShapeDtypeStruct((F, V, R, 4 * PAIRS), jnp.bfloat16),
                          in_specs=[VMEM], out_specs=VMEM, compiler_params=params(12), cost_estimate=cost(SLAB, PAIRS * 4, 2 * KP),
                          name="unpack")(b)


def coef(low, lev, gamma, beta, points):
    return pl.pallas_call(
        coef_kernel, out_shape=(jax.ShapeDtypeStruct((SLABS, 2, SLAB), jnp.float32),
                                jax.ShapeDtypeStruct((2, SLABS, 128), jnp.float32)),
        in_specs=[SMEM] * 4 + [VMEM], out_specs=(VMEM,) * 2, compiler_params=params(8),
        name="coef")(low, lev, gamma, beta, points)


def like(tab):
    return jax.ShapeDtypeStruct(tab.shape, tab.dtype)


def weigh(y, scale):
    return pl.pallas_call(
        weigh_kernel, out_shape=jax.ShapeDtypeStruct((SLABS, COLS, SLAB), jnp.bfloat16),
        in_specs=[VMEM, VMEM], out_specs=VMEM, compiler_params=params(8),
        cost_estimate=cost(SLABS * 128, SLAB, 128), name="weigh")(y, scale)


def pass_on(token, tab):
    return pl.pallas_call(pass_kernel, out_shape=like(tab), in_specs=[ANY, ANY], out_specs=ANY,
                          input_output_aliases={1: 0}, compiler_params=params(1), name="pass_on")(token, tab)


RAW = jax.ShapeDtypeStruct((COLS, KP), jnp.float32)


TURNED = jax.ShapeDtypeStruct((KP, SLAB), jnp.bfloat16)


def near(lev, w, tabs):
    return pl.pallas_call(
        near_kernel, out_shape=(RAW,) + (TURNED,) * NEARS + (like(tabs[0]),),
        in_specs=[SMEM, VMEM] + [ANY] * NEARS, out_specs=(VMEM,) * (2 + NEARS),
        scratch_shapes=[pltpu.VMEM((NEARS - 1, SLAB, KP), jnp.bfloat16), pltpu.SemaphoreType.DMA((NEARS,))],
        compiler_params=params(12), cost_estimate=pl.CostEstimate(flops=NEAR, bytes_accessed=0, transcendentals=0),
        name="near")(lev, w, *tabs)


def far(lev, w, raw, tabs):
    return pl.pallas_call(
        far_kernel, out_shape=(RAW,) + (TURNED,) * FARS, in_specs=[SMEM] + [VMEM] * (2 + FARS),
        out_specs=(VMEM,) * (1 + FARS),
        compiler_params=params(8), cost_estimate=cost(COLS, 4 * SLAB, KP), name="far")(lev, w, raw, *tabs)


def solve(low, lev, level, w, scale, raw, tabs):
    return pl.pallas_call(
        solve_kernel, out_shape=chunks(), in_specs=[SMEM] * 2 + [VMEM] * (4 + len(tabs)), out_specs=VMEM,
        scratch_shapes=[pltpu.VMEM((2, PAIRS, HALF), jnp.float32)],
        compiler_params=params(12), cost_estimate=cost(COLS, 9 * SLAB, KP),
        name="solve")(low, lev, level, w, scale, raw, *tabs)


def along_x(array, step):
    return lax.ppermute(array, "lev", [(d, (d + 2 * step * (1 - 2 * (d % 2))) % SLABS) for d in range(SLABS)])


def other_core(array):
    return lax.ppermute(array, "lev", [(d, d ^ 1) for d in range(SLABS)])


def local(fourier_in, table, points, pair_low, gamma, beta):
    lev = lax.axis_index("lev").astype(jnp.int32).reshape(1)
    own = jnp.swapaxes(table, 1, 2)[0]
    first = along_x(own, 1)
    sent, copied = pack(fourier_in, own)
    second = along_x(copied, -1)
    moved = lax.all_to_all(sent, "wave", split_axis=0, concat_axis=0, tiled=True)
    scale, level = coef(pair_low, lev, gamma, beta, points.reshape(1, NLAT))
    first = pass_on(sent, first)
    third = along_x(first, 1)
    second = pass_on(sent, second)
    cores = [other_core(first), other_core(second)]
    weighted = weigh(moved, scale)
    raw, *tabs, own = near(lev, weighted, [own, first, second])
    third = pass_on(raw, third)
    last = other_core(third)
    raw, *more = far(lev, weighted, raw, [other_core(own)] + cores + [third])
    tabs += more + [last]
    result = solve(pair_low, lev, level, weighted, scale, raw, tabs)
    back = lax.all_to_all(result, "wave", split_axis=0, concat_axis=0, tiled=True)
    return unpack(back)


def solution(mesh):
    placed = (P(None, "lev", "wave", None), P("wave", None, "lev"), P(), P("wave"), P(), P())
    return jax.shard_map(
        local, mesh=mesh, in_specs=placed, out_specs=P(None, "lev", "wave", None), check_vma=False
    )
```

```python
import jax
import jax.numpy as jnp
from jax import lax
from jax.experimental import pallas as pl
from jax.experimental.pallas import tpu as pltpu
from jax.sharding import PartitionSpec as P

F = 2
V = 4
R = 40
PAIRS = 64
SLABS = 8
SLAB = 320
KP = 1281
CUT = KP - 2
NLAT = 2560
STEPS = R // 4
COLS = 32
HALF = 640
NEAR = 73 * 10**8
NEARS = 3
PARTS = 4
FARS = 4

NT = (((1,), (1,)), ((), ()))
NN = (((1,), (0,)), ((), ()))
TN = (((0,), (0,)), ((), ()))
VMEM = pl.BlockSpec(memory_space=pltpu.VMEM)
ANY = pl.BlockSpec(memory_space=pl.ANY)
SMEM = pl.BlockSpec(memory_space=pltpu.SMEM)


def iota(shape, dim):
    return lax.broadcasted_iota(jnp.int32, shape, dim)


def ones_where(cond):
    return jnp.where(cond, 1.0, 0.0).astype(jnp.bfloat16)


def mul(a, b, dims):
    return lax.dot_general(a, b, dims, preferred_element_type=jnp.float32)


def by_member():
    row = iota((4 * PAIRS, 4 * PAIRS), 0)
    return ones_where(iota((4 * PAIRS, 4 * PAIRS), 1) == 4 * (row & (PAIRS - 1)) + (row >> 6))


def by_place():
    lane = iota((1, STEPS * 128), 1)
    source = ((lane >> 3) & 1) * V + ((lane >> 1) & 3)
    source = source * R + 4 * (lane >> 7) + ((lane >> 5) & 3)
    return ones_where(iota((F * V * R, STEPS * 128), 0) == source)


def lane_part(shape):
    lane = iota(shape, 1)
    return ((lane >> 4) & 1) * 2 + (lane & 1)


def pack_kernel(x_ref, tab_ref, o_ref, copy_ref, held_x, held_tab, sems):
    get_x = pltpu.make_async_copy(x_ref, held_x, sems.at[0])
    get_x.start()
    parts = [pl.ds(n * SLAB // PARTS, SLAB // PARTS) for n in range(PARTS)]
    gets = [pltpu.make_async_copy(tab_ref.at[p], held_tab.at[p], sems.at[1 + n]) for n, p in enumerate(parts)]
    puts = [pltpu.make_async_copy(held_tab.at[p], copy_ref.at[p], sems.at[1 + PARTS + n]) for n, p in enumerate(parts)]
    for get in gets:
        get.start()
    get_x.wait()
    x = held_x[...].astype(jnp.float32).reshape(F * V * R, 4 * PAIRS).astype(jnp.bfloat16)
    turned = mul(by_member(), x, NT).astype(jnp.bfloat16)
    for get, put in zip(gets, puts):
        get.wait()
        put.start()
    placed = mul(turned, by_place(), NN)
    part = lane_part((PAIRS, STEPS * 128))
    out = placed[:PAIRS]
    for q in range(1, 4):
        out = jnp.where(part == q, placed[q * PAIRS:(q + 1) * PAIRS], out)
    halves = jnp.stack([out[:, :HALF], out[:, HALF:]], axis=0)
    o_ref[...] = jnp.swapaxes(halves, 0, 1).astype(jnp.bfloat16)
    for put in puts:
        put.wait()


def unpack_kernel(b_ref, o_ref):
    b = jnp.swapaxes(b_ref[...].astype(jnp.float32), 0, 1)
    b = jnp.concatenate([b[0], b[1]], axis=1)
    part = lane_part((PAIRS, STEPS * 128))
    parts = [jnp.where(part == q, b, 0.0).astype(jnp.bfloat16) for q in range(4)]
    turned = mul(by_place(), jnp.concatenate(parts, axis=0), NT).astype(jnp.bfloat16)
    x = mul(turned, by_member(), NN)
    o_ref[...] = x.reshape(F, V, R, 4 * PAIRS).astype(jnp.bfloat16)


def spread_rows():
    row = iota((STEPS * SLABS, SLAB), 0)
    gap = iota((STEPS * SLABS, SLAB), 1) - (row & 7) * R - 4 * (row >> 3)
    return ones_where((gap >= 0) & (gap < 4))


def place_rows():
    lane = iota((1, 512), 1)
    row = (lane & 7) * R + 4 * ((lane >> 3) & 15) + (lane >> 7)
    return ones_where((iota((SLAB, 512), 0) == row) & (((lane >> 3) & 15) < STEPS))


def own_group():
    return (iota((4 * COLS, SLAB), 0) >> 5) == (iota((4 * COLS, SLAB), 1) & 3)


def coef_kernel(low_ref, lev_ref, gamma_ref, beta_ref, points_ref, scale_ref, level_ref):
    low = low_ref[0]
    points = jnp.concatenate([points_ref[:, s * SLAB:(s + 1) * SLAB] for s in range(SLABS)], axis=0)
    pts = points.astype(jnp.float32)
    weights = NLAT * pts / jnp.sum(pts)
    limit = jnp.minimum(CUT, (points >> 1) - 1)
    rows = jnp.stack([jnp.where(low <= limit, weights, 0.0), jnp.where(CUT - low <= limit, weights, 0.0)], axis=0)
    for s in range(SLABS):
        scale_ref[s] = rows[:, s, :]
    level = iota((SLABS, 128), 0) >> 1
    gval = jnp.zeros((SLABS, 128), jnp.float32)
    bval = jnp.zeros((SLABS, 128), jnp.float32)
    for v in range(V):
        gval = jnp.where(level == v, gamma_ref[lev_ref[0] * V + v], gval)
        bval = jnp.where(level == v, beta_ref[lev_ref[0] * V + v], bval)
    level_ref[0] = gval
    level_ref[1] = bval


def members(pair):
    return jnp.concatenate([jnp.broadcast_to(pair[m:m + 1], (COLS // 2, SLAB)) for m in range(2)], axis=0)


def weigh_kernel(y_ref, scale_ref, o_ref):
    spread = spread_rows()
    group = own_group()
    y = jnp.swapaxes(y_ref[...].astype(jnp.float32), 0, 1)
    for s in range(SLABS):
        rows = y[:, s * SLABS:(s + 1) * SLABS]
        block = jnp.concatenate([rows[j // 5, :, (j % 5) * 128:(j % 5 + 1) * 128] for j in range(STEPS)], axis=0)
        turned = jnp.where(group, mul(block.astype(jnp.bfloat16), spread, TN), 0.0)
        turned = turned[:32] + turned[32:64] + turned[64:96] + turned[96:]
        o_ref[s] = (turned * members(scale_ref[s])).astype(jnp.bfloat16)


def slab_order(lev):
    way = 2 - 4 * (lev & 1)
    behind, ahead, far = (lev - way) & 7, (lev + way) & 7, lev ^ 4
    return [lev, behind, ahead, lev ^ 1, ahead ^ 1, behind ^ 1, far, far ^ 1]


def add_up(raw, w_ref, slabs, tabs):
    for slab, tab in zip(slabs, tabs):
        term = mul(w_ref[slab], tab[...], NN)
        raw = term if raw is None else raw + term
    return raw


def near_kernel(lev_ref, w_ref, *refs):
    tabs, raw_ref, turned, same_ref, held, sems = refs[:NEARS], refs[NEARS], refs[NEARS + 1:-3], *refs[-3:]
    places = [same_ref] + [held.at[n] for n in range(NEARS - 1)]
    copies = [pltpu.make_async_copy(tabs[n], places[n], sems.at[n]) for n in range(NEARS)]
    for copy in copies:
        copy.start()
    slabs = slab_order(lev_ref[0])
    raw = None
    for n in range(NEARS):
        copies[n].wait()
        raw = add_up(raw, w_ref, slabs[n:n + 1], places[n:n + 1])
        turned[n][...] = places[n][...].T
    raw_ref[...] = raw


def far_kernel(lev_ref, w_ref, raw_ref, *refs):
    tabs, total_ref, turned = refs[:FARS], refs[FARS], refs[FARS + 1:]
    total_ref[...] = add_up(raw_ref[...], w_ref, slab_order(lev_ref[0])[NEARS:], tabs)
    for tab, turn in zip(tabs, turned):
        turn[...] = tab[...].T


def pass_kernel(token_ref, tab_ref, same_ref):
    pass


def solve_kernel(low_ref, lev_ref, level_ref, w_ref, scale_ref, raw_ref, *refs):
    *tabs, o_ref, out_ref = refs
    low = low_ref[0]
    slabs = slab_order(lev_ref[0])
    wide = add_up(raw_ref[...], w_ref, slabs[7:], tabs[7:])
    kidx = iota((1, KP), 1)
    first = kidx <= CUT - low
    degree = jnp.where(first, low + kidx, kidx - 1).astype(jnp.float32)
    eig = degree * (degree + 1.0) / (CUT * (CUT + 1.0))
    gval = level_ref[0, :, 0:1]
    bval = level_ref[1, :, 0:1]
    spectra = jnp.where(first, wide[:16], wide[16:])
    drive, mass = spectra[:8], spectra[8:]
    solved = (drive - bval * eig * mass) / (1.0 + gval * eig)
    spec = jnp.concatenate([solved, mass + bval * solved], axis=0)
    expanded = jnp.concatenate([jnp.where(first, spec, 0.0), jnp.where(first, 0.0, spec)], axis=0).astype(jnp.bfloat16)
    rows = []
    for n, slab in enumerate(slabs):
        part = mul(expanded, tabs[n][...], NN if n < NEARS + FARS else NT)
        rows.append(jnp.where(members(scale_ref[slab]) > 0.0, part, 0.0).astype(jnp.bfloat16))
    placed = mul(jnp.concatenate(rows, axis=0), place_rows(), NN)
    for n, slab in enumerate(slabs):
        part = placed[n * COLS:(n + 1) * COLS]
        block = jnp.concatenate([part[:, g * 128:(g + 1) * 128] for g in range(4)], axis=0).T
        place = pl.ds(pl.multiple_of(slab * SLABS, SLABS), SLABS)
        for j in range(STEPS):
            out_ref[j // 5, place, (j % 5) * 128:(j % 5 + 1) * 128] = block[j * SLABS:(j + 1) * SLABS]
    o_ref[...] = jnp.swapaxes(out_ref[...], 0, 1).astype(jnp.bfloat16)


def params(mib):
    return pltpu.CompilerParams(vmem_limit_bytes=mib * 1024 * 1024)


def cost(rows, depth, columns):
    return pl.CostEstimate(flops=2 * max(rows, 256) * depth * columns, transcendentals=0,
                           bytes_accessed=2 * depth * columns)


def chunks():
    return jax.ShapeDtypeStruct((PAIRS, 2, HALF), jnp.bfloat16)


def pack(x, tab):
    return pl.pallas_call(
        pack_kernel, out_shape=(chunks(), like(tab)), in_specs=[ANY, ANY], out_specs=(VMEM, ANY),
        scratch_shapes=[pltpu.VMEM(x.shape, x.dtype), pltpu.VMEM(tab.shape, tab.dtype), pltpu.SemaphoreType.DMA((1 + 2 * PARTS,))],
        compiler_params=params(60), cost_estimate=cost(PAIRS * 4, SLAB, 2 * KP), name="pack")(x, tab)


def unpack(b):
    return pl.pallas_call(unpack_kernel, out_shape=jax.ShapeDtypeStruct((F, V, R, 4 * PAIRS), jnp.bfloat16),
                          in_specs=[VMEM], out_specs=VMEM, compiler_params=params(12), cost_estimate=cost(SLAB, PAIRS * 4, 2 * KP),
                          name="unpack")(b)


def coef(low, lev, gamma, beta, points):
    return pl.pallas_call(
        coef_kernel, out_shape=(jax.ShapeDtypeStruct((SLABS, 2, SLAB), jnp.float32),
                                jax.ShapeDtypeStruct((2, SLABS, 128), jnp.float32)),
        in_specs=[SMEM] * 4 + [VMEM], out_specs=(VMEM,) * 2, compiler_params=params(8),
        name="coef")(low, lev, gamma, beta, points)


def like(tab):
    return jax.ShapeDtypeStruct(tab.shape, tab.dtype)


def weigh(y, scale):
    return pl.pallas_call(
        weigh_kernel, out_shape=jax.ShapeDtypeStruct((SLABS, COLS, SLAB), jnp.bfloat16),
        in_specs=[VMEM, VMEM], out_specs=VMEM, compiler_params=params(8),
        cost_estimate=cost(SLABS * 128, SLAB, 128), name="weigh")(y, scale)


def pass_on(token, tab):
    return pl.pallas_call(pass_kernel, out_shape=like(tab), in_specs=[ANY, ANY], out_specs=ANY,
                          input_output_aliases={1: 0}, compiler_params=params(1), name="pass_on")(token, tab)


RAW = jax.ShapeDtypeStruct((COLS, KP), jnp.float32)


TURNED = jax.ShapeDtypeStruct((KP, SLAB), jnp.bfloat16)


def near(lev, w, tabs):
    return pl.pallas_call(
        near_kernel, out_shape=(RAW,) + (TURNED,) * NEARS + (like(tabs[0]),),
        in_specs=[SMEM, VMEM] + [ANY] * NEARS, out_specs=(VMEM,) * (2 + NEARS),
        scratch_shapes=[pltpu.VMEM((NEARS - 1, SLAB, KP), jnp.bfloat16), pltpu.SemaphoreType.DMA((NEARS,))],
        compiler_params=params(12), cost_estimate=pl.CostEstimate(flops=NEAR, bytes_accessed=0, transcendentals=0),
        name="near")(lev, w, *tabs)


def far(lev, w, raw, tabs):
    return pl.pallas_call(
        far_kernel, out_shape=(RAW,) + (TURNED,) * FARS, in_specs=[SMEM] + [VMEM] * (2 + FARS),
        out_specs=(VMEM,) * (1 + FARS),
        compiler_params=params(8), cost_estimate=cost(COLS, 4 * SLAB, KP), name="far")(lev, w, raw, *tabs)


def solve(low, lev, level, w, scale, raw, tabs):
    return pl.pallas_call(
        solve_kernel, out_shape=chunks(), in_specs=[SMEM] * 2 + [VMEM] * (4 + len(tabs)), out_specs=VMEM,
        scratch_shapes=[pltpu.VMEM((2, PAIRS, HALF), jnp.float32)],
        compiler_params=params(12), cost_estimate=cost(COLS, 9 * SLAB, KP),
        name="solve")(low, lev, level, w, scale, raw, *tabs)


def along_x(array, step):
    return lax.ppermute(array, "lev", [(d, (d + 2 * step * (1 - 2 * (d % 2))) % SLABS) for d in range(SLABS)])


def other_core(array):
    return lax.ppermute(array, "lev", [(d, d ^ 1) for d in range(SLABS)])


def local(fourier_in, table, points, pair_low, gamma, beta):
    lev = lax.axis_index("lev").astype(jnp.int32).reshape(1)
    own = jnp.swapaxes(table, 1, 2)[0]
    first = along_x(own, 1)
    sent, copied = pack(fourier_in, own)
    second = along_x(copied, -1)
    moved = lax.all_to_all(sent, "wave", split_axis=0, concat_axis=0, tiled=True)
    scale, level = coef(pair_low, lev, gamma, beta, points.reshape(1, NLAT))
    first = pass_on(sent, first)
    third = along_x(first, 1)
    second = pass_on(sent, second)
    cores = [other_core(first), other_core(second)]
    weighted = weigh(moved, scale)
    raw, *tabs, own = near(lev, weighted, [own, first, second])
    third = pass_on(raw, third)
    last = other_core(third)
    raw, *more = far(lev, weighted, raw, [other_core(own)] + cores + [third])
    tabs += more + [last]
    result = solve(pair_low, lev, level, weighted, scale, raw, tabs)
    back = lax.all_to_all(result, "wave", split_axis=0, concat_axis=0, tiled=True)
    return unpack(back)


def solution(mesh):
    placed = (P(None, "lev", "wave", None), P("wave", None, "lev"), P(), P("wave"), P(), P())
    return jax.shard_map(
        local, mesh=mesh, in_specs=placed, out_specs=P(None, "lev", "wave", None), check_vma=False
    )
```
